32 devices in a mesh: node: 8 (over z, y), rep: 4 (over x, core).
Axes of the slice: x: 2, y: 2, z: 4, core: 2. Of those that a mesh axis runs over, the one named last changes fastest.
Arguments:
- memory: float32 [8192, 256], P('node'), may hold values from -3 to 3
- hot_memory: float32 [1024, 256], replicated, may hold values from -3 to 3
- cot_cold: float32 [8192, 256], P('node'), may hold values from -6 to 6
- cot_hot: float32 [1024, 256], replicated, may hold values from -6 to 6
- src_local: int32 [32768], P(('node', 'rep')), may hold values from 0 to 1023
- dst_ids: int32 [32768], P(('node', 'rep')), may hold values from 0 to 9215, as said below
- times: int32 [32768], P(('node', 'rep')), may hold values from 0 to 4095
- edge_feat: bfloat16 [32768, 128], P(('node', 'rep')), may hold values from -6 to 6
- cold_list: int32 [256, 128], P(('node', 'rep')), may hold values from 0 to 1023, as said below
- cold_count: int32 [256], P(('node', 'rep')), may hold values from 0 to 128, as said below
- hot_ids: int32 [1024], replicated, may hold values from 8192 to 9215, as said below
- time_freq: float32 [128], replicated, may hold values from 0.001 to 1
- time_phase: float32 [128], replicated, may hold values from -3.140625 to 3.140625
- w_msg: bfloat16 [512, 512], replicated, may hold values from -0.25 to 0.25
- b_msg: float32 [512], replicated, may hold values from -3 to 3
- w_in: bfloat16 [512, 768], replicated, may hold values from -0.25 to 0.25
- w_hid: bfloat16 [256, 768], replicated, may hold values from -0.375 to 0.375
Outputs:
- new_memory: float32 [8192, 256], P('node')
- new_hot: float32 [1024, 256], replicated
- grad_in: float32 [512, 768], replicated
- grad_hid: float32 [256, 768], replicated
The draws below stay inside these ranges and needn't reach their ends.
Inputs may be any that keep to these rules, and one draw needn't show every extreme that they name: `dst_ids`: each device's events split into cold ones, each named in exactly one used slot of its owner's list, and hot ones whose destination is in hot_ids; cold destinations are node ids below 8192, hot ones 8192 or more. The hot destinations of device d are among the ids 8192 + ((d * 32 + j) mod 1024) for j below 128. `cold_list`: used slots hold distinct event indices of the device; unused slots hold 0. `cold_count`: some owner's list is full on every device. `hot_ids`: A permutation of the hot node ids 8192 to 9215.
All inputs are finite; a program needn't handle non-finite values.
Results may differ from the reference program's by a relative error of at most 0.0018.
The reference program's roundings to bfloat16 on the way (of `src_mem`, `enc`, `messages` and `agg`) count: a program that leaves them out, or rounds other values in their place, can miss the bound.
Values may be sent and summed in bfloat16 or wider, within the bound.
A program may use at most 128 MiB of HBM per device.

```python
import math
import jax
import jax.numpy as jnp
from jax import lax

DM = 256
EF = 128
TE = 128
MSG = 512
HOT = 1024
NODES_DEV = 1024
E_DEV = 1024
T_BINS = 4096
CAP = 128
NODES = 8192
EVENTS = 32768
N_NODE = 8
N_REP = 4


def event_plan(key):
    key_heavy, key_light, key_big, key_perm, key_row, key_hot = jax.random.split(key, 6)
    devices = N_NODE * N_REP
    heavy = jax.random.permutation(key_heavy, N_NODE)[:4]
    is_heavy = jnp.zeros((N_NODE,), jnp.int32).at[heavy].set(1)
    light = jax.random.randint(key_light, (devices, N_NODE), CAP // 8, CAP // 2 + 1)
    big = jax.random.randint(key_big, (devices, N_NODE), 3 * CAP // 4, CAP + 1)
    counts = jnp.where(is_heavy[None, :] == 1, big, light)
    counts = counts.at[:, heavy[0]].set(CAP)
    ends = jnp.cumsum(counts, axis=1)
    starts = ends - counts
    perms = jax.vmap(lambda k: jax.random.permutation(k, E_DEV))(jax.random.split(key_perm, devices)).astype(jnp.int32)
    slots = jnp.arange(CAP, dtype=jnp.int32)
    valid = slots[None, None, :] < counts[:, :, None]
    where_at = jnp.where(valid, starts[:, :, None] + slots[None, None, :], 0).reshape(devices, N_NODE * CAP)
    lists = jnp.take_along_axis(perms, where_at, axis=1).reshape(devices, N_NODE, CAP)
    lists = jnp.where(valid, lists, 0)
    place = jnp.arange(E_DEV, dtype=jnp.int32)
    owner_at = jnp.sum((place[None, :, None] >= ends[:, None, :]).astype(jnp.int32), axis=2)
    cold_at = place[None, :] < ends[:, -1:]
    rows = jax.random.randint(key_row, (devices, E_DEV), 0, NODES_DEV)
    band = HOT // devices
    offsets = jax.random.randint(key_hot, (devices, E_DEV), 0, 4 * band)
    firsts = jnp.arange(devices, dtype=jnp.int32)[:, None] * band
    hots = NODES + (firsts + offsets) % HOT
    dst_at = jnp.where(cold_at, jnp.minimum(owner_at, N_NODE - 1) * NODES_DEV + rows, hots)
    dst = jax.vmap(lambda p, v: jnp.zeros((E_DEV,), jnp.int32).at[p].set(v))(perms, dst_at.astype(jnp.int32))
    return (counts.astype(jnp.int32), lists.astype(jnp.int32), dst)


def draw_dst_ids(key, part):
    counts, lists, dst = event_plan(key)
    return dst.reshape(-1)


def draw_cold_list(key, part):
    counts, lists, dst = event_plan(key)
    return lists.reshape(N_NODE * N_REP * N_NODE, CAP)


def draw_cold_count(key, part):
    counts, lists, dst = event_plan(key)
    return counts.reshape(-1)


def draw_hot_ids(key, part):
    key = jax.random.fold_in(key, 7)
    return (NODES + jax.random.permutation(key, HOT)).astype(jnp.int32)


def plant(values, key, smallest, high):
    spot = [jax.random.randint(jax.random.fold_in(key, axis), (), 0, length) for axis, length in enumerate(values.shape)]
    longest = values.shape.index(max(values.shape))
    neighbour = spot[:longest] + [(spot[longest] + 1) % values.shape[longest]] + spot[longest + 1:]
    return values.at[tuple(spot)].set(smallest).at[tuple(neighbour)].set(high)


def block_levels(own_key, dims, cuts, low, top_value):
    loudness = 1.0
    for dim, blocks in cuts:
        steps = jax.random.uniform(jax.random.fold_in(jax.random.fold_in(own_key, 6), dim), (blocks,), jnp.float32, low / len(cuts), top_value / len(cuts))
        loudness = loudness * jnp.repeat(jnp.exp(steps), dims[dim] // blocks).reshape((-1,) + (1,) * (len(dims) - 1 - dim))
    return loudness


def normal_values(own_key, shape, spread, reach, pieces=(), kind=jnp.bfloat16):
    array = spread * jax.random.normal(own_key, shape, jnp.float32)
    if pieces:
        array = array * block_levels(own_key, shape, pieces, -0.22, 0.18)
    return jnp.clip(array, -reach, reach).astype(kind)


def setup_inputs(seed: int = 0) -> dict:
    arg_keys = jax.random.split(jax.random.key(seed), 18)
    return {
        "memory": normal_values(arg_keys[0], (NODES, DM), 0.5, 3.0, ((0, 8),), jnp.float32),
        "hot_memory": normal_values(arg_keys[1], (HOT, DM), 0.5, 3.0, (), jnp.float32),
        "cot_cold": normal_values(arg_keys[2], (NODES, DM), 1.0, 6.0, ((0, 8),), jnp.float32),
        "cot_hot": normal_values(arg_keys[3], (HOT, DM), 1.0, 6.0, (), jnp.float32),
        "src_local": plant(jax.random.randint(arg_keys[4], (EVENTS,), 0, NODES_DEV), jax.random.fold_in(arg_keys[4], 1), 0, NODES_DEV - 1).astype(jnp.int32),
        "dst_ids": draw_dst_ids(jax.random.fold_in(arg_keys[17], 71), 0),
        "times": plant(jax.random.randint(arg_keys[6], (EVENTS,), 0, T_BINS), jax.random.fold_in(arg_keys[6], 1), 0, T_BINS - 1).astype(jnp.int32),
        "edge_feat": normal_values(arg_keys[7], (EVENTS, EF), 1.0, 6.0, ((0, 32),)),
        "cold_list": draw_cold_list(jax.random.fold_in(arg_keys[17], 71), 0),
        "cold_count": draw_cold_count(jax.random.fold_in(arg_keys[17], 71), 0),
        "hot_ids": draw_hot_ids(jax.random.fold_in(arg_keys[17], 71), 0),
        "time_freq": jnp.clip(jnp.exp(jax.random.uniform(arg_keys[11], (TE,), jnp.float32, math.log(0.001), math.log(1.0))), 0.001, 1.0),
        "time_phase": jnp.clip(jax.random.uniform(arg_keys[12], (TE,), jnp.float32, -3.140625, 3.140625), -3.140625, 3.140625),
        "w_msg": normal_values(arg_keys[13], (MSG, MSG), MSG ** -0.5, 0.25),
        "b_msg": normal_values(arg_keys[14], (MSG,), 0.5, 3.0, (), jnp.float32),
        "w_in": normal_values(arg_keys[15], (MSG, 3 * DM), MSG ** -0.5, 0.25),
        "w_hid": normal_values(arg_keys[16], (DM, 3 * DM), DM ** -0.5, 0.375),
    }


GRAD_SCALE = 1.0 / 64.0


def gru_forward(agg, mem, w_in, w_hid):
    width = mem.shape[1]
    gate_in = jnp.dot(agg, w_in, preferred_element_type=jnp.float32)
    gate_hid = jnp.dot(mem.astype(jnp.bfloat16), w_hid, preferred_element_type=jnp.float32)
    reset = jax.nn.sigmoid(gate_in[:, :width] + gate_hid[:, :width])
    update = jax.nn.sigmoid(gate_in[:, width:2 * width] + gate_hid[:, width:2 * width])
    cand = jnp.tanh(gate_in[:, 2 * width:] + reset * gate_hid[:, 2 * width:])
    fresh = (1.0 - update) * cand + update * mem
    return fresh, (reset, update, cand, gate_hid[:, 2 * width:])


def gru_grads(agg, mem, saved, cot):
    reset, update, cand, hid_cand = saved
    d_cand = cot * (1.0 - update) * (1.0 - cand * cand)
    d_upd = cot * (mem - cand) * update * (1.0 - update)
    d_reset = d_cand * hid_cand * reset * (1.0 - reset)
    d_input = jnp.concatenate([d_reset, d_upd, d_cand], axis=1)
    d_hidden = jnp.concatenate([d_reset, d_upd, d_cand * reset], axis=1)
    mem_round = lax.optimization_barrier(mem.astype(jnp.bfloat16)).astype(jnp.float32)
    grad_a = jnp.dot(agg.astype(jnp.float32).T, d_input, precision=lax.Precision.HIGHEST)
    grad_b = jnp.dot(mem_round.T, d_hidden, precision=lax.Precision.HIGHEST)
    return grad_a, grad_b


def update_rows(total, count, mem, cot, w_in, w_hid):
    agg = (total / jnp.maximum(count, 1.0)[:, None]).astype(jnp.bfloat16)
    fresh, saved = gru_forward(agg, mem, w_in, w_hid)
    live = (count > 0)[:, None]
    result = jnp.where(live, fresh, mem)
    grad_a, grad_b = gru_grads(agg, mem, saved, jnp.where(live, cot, 0.0))
    return result, grad_a, grad_b


def reference(memory, hot_memory, cot_cold, cot_hot, src_local, dst_ids, times, edge_feat, cold_list, cold_count, hot_ids, time_freq, time_phase, w_msg, b_msg, w_in, w_hid):
    devices = N_NODE * N_REP
    owner_base = (jnp.arange(devices, dtype=jnp.int32) // N_REP) * NODES_DEV
    src_global = (owner_base[:, None] + src_local.reshape(devices, E_DEV)).reshape(-1)
    src_mem = jnp.take(memory, src_global, axis=0).astype(jnp.bfloat16)
    enc = jnp.cos(times.astype(jnp.float32)[:, None] * time_freq[None, :] + time_phase[None, :]).astype(jnp.bfloat16)
    raw = jnp.concatenate([src_mem, edge_feat, enc], axis=1)
    messages = jax.nn.silu(jnp.dot(raw, w_msg, preferred_element_type=jnp.float32) + b_msg[None, :]).astype(jnp.bfloat16)
    lists = cold_list.reshape(devices, N_NODE * CAP)
    slots = jnp.arange(CAP, dtype=jnp.int32)
    valid = (slots[None, :] < cold_count[:, None]).reshape(devices, N_NODE * CAP)
    event_idx = (jnp.arange(devices, dtype=jnp.int32)[:, None] * E_DEV + lists).reshape(-1)
    seg = jnp.where(valid.reshape(-1), jnp.take(dst_ids, event_idx), NODES).astype(jnp.int32)
    picked = jnp.take(messages, event_idx, axis=0).astype(jnp.float32)
    cold_total = jax.ops.segment_sum(picked, seg, num_segments=NODES + 1)[:NODES]
    cold_cnt = jax.ops.segment_sum(jnp.ones(seg.shape, jnp.float32), seg, num_segments=NODES + 1)[:NODES]
    inverse = jnp.zeros((HOT,), jnp.int32).at[hot_ids - NODES].set(jnp.arange(HOT, dtype=jnp.int32))
    is_hot = dst_ids >= NODES
    hot_seg = jnp.where(is_hot, jnp.take(inverse, jnp.clip(dst_ids - NODES, 0, HOT - 1)), HOT).astype(jnp.int32)
    hot_total = jax.ops.segment_sum(messages.astype(jnp.float32), hot_seg, num_segments=HOT + 1)[:HOT]
    hot_cnt = jax.ops.segment_sum(jnp.ones(hot_seg.shape, jnp.float32), hot_seg, num_segments=HOT + 1)[:HOT]
    new_memory, grad_a, grad_b = update_rows(cold_total, cold_cnt, memory, cot_cold, w_in, w_hid)
    new_hot, hot_a, hot_b = update_rows(hot_total, hot_cnt, hot_memory, cot_hot, w_in, w_hid)
    return new_memory, new_hot, (grad_a + hot_a) * GRAD_SCALE, (grad_b + hot_b) * GRAD_SCALE
```

```python
import functools

import jax
import jax.numpy as jnp
from jax import lax
from jax.experimental import pallas as pl
from jax.experimental.pallas import tpu as pltpu
from jax.sharding import PartitionSpec as P

GRAD_SCALE = 1.0 / 64.0
BANDS = 4
MESH = pl.DeviceIdType.MESH
VMEM = pl.BlockSpec(memory_space=pltpu.VMEM)


def greet(devices):
    barrier = pltpu.get_barrier_semaphore()
    for device in devices:
        pl.semaphore_signal(barrier, inc=1, device_id=device, device_id_type=MESH)
    pl.semaphore_wait(barrier, len(devices))


def push(src, dst, send_sem, recv_sem, device):
    copy = pltpu.make_async_remote_copy(
        src_ref=src, dst_ref=dst, send_sem=send_sem, recv_sem=recv_sem, device_id=device, device_id_type=MESH
    )
    copy.start()
    return copy


def exchange_kernel(
    n_node, n_rep,
    msg_ref, rows_ref, hot_ref,
    sum_out, cnt_out, hot_out,
    msg_recv, rows_recv, hot_recv, sums, cnts, core_recv, x_send, x_recv, cnt_core, cnt_send, cnt_x,
    msg_s, msg_r, row_s, row_r, hot_s, hot_r, core_s, core_r, x_s, x_r, cc_s, cc_r, cx_s, cx_r,
):
    nx = n_rep // 2
    n_dev = n_node * n_rep
    node = lax.axis_index("node")
    rep = lax.axis_index("rep")
    core = lax.rem(rep, 2)
    xi = lax.div(rep, 2)
    me = node * n_rep + rep
    cap = msg_ref.shape[1]
    share = sum_out.shape[0]

    def at_node(k):
        return (lax.rem(node + k, n_node), rep)

    def at_linear(k):
        other = lax.rem(me + k, n_dev)
        return (lax.div(other, n_rep), lax.rem(other, n_rep))

    other_core = (node, xi * 2 + 1 - core)

    def at_x(k):
        return (node, lax.rem(xi + k, nx) * 2 + core)

    greet(
        [at_node(k) for k in range(1, n_node)]
        + [other_core]
        + [at_x(k) for k in range(1, nx)]
        + [at_linear(j) for j in range(1, BANDS)]
        + [at_linear(n_dev - j) for j in range(1, BANDS)]
    )

    sent = []
    arrivals = {}
    for k in range(1, n_node):
        other = lax.rem(node + k, n_node)
        row = push(rows_ref.at[other], rows_recv.at[node], row_s.at[k], row_r.at[k], at_node(k))
        msg = push(msg_ref.at[other], msg_recv.at[node], msg_s.at[k], msg_r.at[k], at_node(k))
        arrivals[k] = (row, msg)
        sent += [row, msg]
    hots = [
        push(hot_ref.at[j], hot_recv.at[j - 1], hot_s.at[j - 1], hot_r.at[j - 1], at_linear(j))
        for j in range(1, BANDS)
    ]
    sent += hots

    sums[...] = jnp.zeros_like(sums)
    cnts[...] = jnp.zeros_like(cnts)
    ones = jnp.ones((8, cap), jnp.bfloat16)

    def add_block(rows, block):
        for s in range(n_rep):
            spot = lax.broadcasted_iota(jnp.int32, (share, cap), 0) + s * share
            equal = jnp.where(spot == rows, 1.0, 0.0).astype(jnp.bfloat16)
            sums[s // 2, s % 2] += jnp.dot(equal, block, preferred_element_type=jnp.float32)
            cnts[s] += lax.dot_general(
                ones, equal, (((1,), (1,)), ((), ())), preferred_element_type=jnp.float32
            )

    add_block(rows_ref[node, 0:1, :cap], msg_ref[node])
    for k in range(1, n_node):
        row, msg = arrivals[k]
        row.wait_recv()
        msg.wait_recv()
        origin = lax.rem(node + n_node - k, n_node)
        add_block(rows_recv[origin, 0:1, :cap], msg_recv[origin])

    halves = []
    for k in [*range(1, nx), 0]:
        p = lax.rem(xi + k, nx)
        halves.append((k, p, push(sums.at[p, 1 - core], core_recv.at[k], core_s.at[k], core_r.at[k], other_core)))
    cnt_copy = push(cnts, cnt_core, cc_s, cc_r, other_core)
    sent.append(cnt_copy)
    crossing = []
    for k, p, copy in halves:
        copy.wait_recv()
        sent.append(copy)
        if k:
            x_send[k - 1] = sums[p, core] + core_recv[k]
            crossing.append(push(x_send.at[k - 1], x_recv.at[k - 1], x_s.at[k - 1], x_r.at[k - 1], at_x(k)))
    cnt_copy.wait_recv()
    cnt_send[...] = cnts[...] + cnt_core[...]
    counts = [
        push(cnt_send, cnt_x.at[k - 1], cx_s.at[k - 1], cx_r.at[k - 1], at_x(k)) for k in range(1, nx)
    ]
    for copy in hots:
        copy.wait_recv()
    hot_out[...] = hot_ref[0] + hot_recv[0] + hot_recv[1] + hot_recv[2]
    total = sums[xi, core] + core_recv[0]
    for k, copy in enumerate(crossing):
        copy.wait_recv()
        total += x_recv[k]
    sum_out[...] = total
    number = cnt_send[...]
    for k, copy in enumerate(counts):
        copy.wait_recv()
        number += cnt_x[k]
    cnt_out[...] = number
    for copy in [*sent, *crossing, *counts]:
        copy.wait_send()


def exchange(n_node, n_rep, rows_dev, msg, rows, hot):
    nx = n_rep // 2
    cap, width = msg.shape[1:]
    band, hot_width = hot.shape[1:]
    share = rows_dev // n_rep
    dma = pltpu.SemaphoreType.DMA
    f32 = jnp.float32
    return pl.pallas_call(
        functools.partial(exchange_kernel, n_node, n_rep),
        out_shape=(
            jax.ShapeDtypeStruct((share, width), f32),
            jax.ShapeDtypeStruct((n_rep, 8, share), f32),
            jax.ShapeDtypeStruct((band, hot_width), f32),
        ),
        in_specs=[VMEM] * 3,
        out_specs=(VMEM,) * 3,
        scratch_shapes=[
            pltpu.VMEM(msg.shape, msg.dtype),
            pltpu.VMEM(rows.shape, rows.dtype),
            pltpu.VMEM((BANDS - 1, band, hot_width), f32),
            pltpu.VMEM((nx, 2, share, width), f32),
            pltpu.VMEM((n_rep, 8, share), f32),
            pltpu.VMEM((nx, share, width), f32),
            pltpu.VMEM((nx - 1, share, width), f32),
            pltpu.VMEM((nx - 1, share, width), f32),
            pltpu.VMEM((n_rep, 8, share), f32),
            pltpu.VMEM((n_rep, 8, share), f32),
            pltpu.VMEM((nx - 1, n_rep, 8, share), f32),
            dma((n_node,)), dma((n_node,)), dma((n_node,)), dma((n_node,)),
            dma((BANDS - 1,)), dma((BANDS - 1,)),
            dma((nx,)), dma((nx,)),
            dma((nx - 1,)), dma((nx - 1,)),
            dma, dma,
            dma((nx - 1,)), dma((nx - 1,)),
        ],
        compiler_params=pltpu.CompilerParams(
            collective_id=0, has_side_effects=True, vmem_limit_bytes=40 * 1024 * 1024
        ),
    )(msg, rows, hot)


ORDER_A = ("core", "x", "lo", "hi")
ORDER_B = ("core", "lo", "x", "hi")


def sizes_of(n_node, n_rep):
    return {"core": 2, "x": n_rep // 2, "lo": n_node // 4, "hi": 4}


def finish_kernel(n_node, n_rep, n_sems, ga_ref, gb_ref, cold_ref, hot_ref, oa, ob, ocold, ohot, *scratch):
    sizes = sizes_of(n_node, n_rep)
    recv_a, acc_a, recv_b, acc_b = scratch[0:4], scratch[4:8], scratch[8:12], scratch[12:16]
    send_sem, recv_sem = scratch[16:18]
    node = lax.axis_index("node")
    rep = lax.axis_index("rep")
    nlo = sizes["lo"]
    mine = {"core": lax.rem(rep, 2), "x": lax.div(rep, 2), "lo": lax.rem(node, nlo), "hi": lax.div(node, nlo)}

    def peer(axis, k):
        spot = dict(mine)
        spot[axis] = lax.rem(mine[axis] + k, sizes[axis])
        return (spot["hi"] * nlo + spot["lo"], spot["x"] * 2 + spot["core"])

    greet([peer(axis, k) for axis in ORDER_A for k in range(1, sizes[axis])])

    used = [0]
    everything = []

    def ship(src, dst, device):
        i = used[0]
        used[0] += 1
        copy = push(src, dst, send_sem.at[i], recv_sem.at[i], device)
        everything.append(copy)
        return copy

    def scatter_start(cur, recv, axis):
        size = sizes[axis]
        return [
            ship(cur.at[lax.rem(mine[axis] + k, size)], recv.at[k - 1], peer(axis, k)) for k in range(1, size)
        ]

    def scatter_end(copies, cur, recv, acc, axis):
        total = cur[mine[axis]]
        for k, copy in enumerate(copies):
            copy.wait_recv()
            total = total + recv[k]
        acc[...] = total

    def gather_start(out, order, phase):
        axis = order[phase]
        where = out.at[tuple(mine[a] for a in order[: phase + 1])]
        return [ship(where, where, peer(axis, k)) for k in range(1, sizes[axis])]

    def arrive(copies):
        for copy in copies:
            copy.wait_recv()

    ocold[mine["x"], mine["core"]] = cold_ref[...]
    ohot[tuple(mine[a] for a in ORDER_A)] = hot_ref[...]
    cold_place = ocold.at[mine["x"], mine["core"]]
    first_a = scatter_start(ga_ref, recv_a[0], ORDER_A[0])
    first_b = scatter_start(gb_ref, recv_b[0], ORDER_B[0])
    cold_copies = [ship(cold_place, cold_place, peer("x", k)) for k in range(1, sizes["x"])]
    hot_copies = gather_start(ohot, ORDER_A, 3)

    cur_a, cur_b, copies_a, copies_b = ga_ref, gb_ref, first_a, first_b
    for phase in range(4):
        scatter_end(copies_a, cur_a, recv_a[phase], acc_a[phase], ORDER_A[phase])
        cur_a = acc_a[phase]
        if phase < 3:
            copies_a = scatter_start(cur_a, recv_a[phase + 1], ORDER_A[phase + 1])
        scatter_end(copies_b, cur_b, recv_b[phase], acc_b[phase], ORDER_B[phase])
        cur_b = acc_b[phase]
        if phase < 3:
            copies_b = scatter_start(cur_b, recv_b[phase + 1], ORDER_B[phase + 1])
        if phase == 0:
            arrive(hot_copies)
            hot_copies = gather_start(ohot, ORDER_A, 2)
        if phase == 1:
            arrive(cold_copies)
            side = ocold.at[:, mine["core"]]
            cold_copies = [ship(side, side, peer("core", 1))]
        if phase == 2:
            arrive(hot_copies)
            hot_copies = gather_start(ohot, ORDER_A, 1)
    oa[tuple(mine[a] for a in ORDER_A)] = cur_a[...]
    ob[tuple(mine[a] for a in ORDER_B)] = cur_b[...]
    for phase in (3, 2, 1, 0):
        copies_a = gather_start(oa, ORDER_A, phase)
        copies_b = gather_start(ob, ORDER_B, phase)
        if phase == 2:
            arrive(hot_copies)
            hot_copies = gather_start(ohot, ORDER_A, 0)
        arrive(copies_a)
        arrive(copies_b)
    arrive(hot_copies)
    arrive(cold_copies)
    for copy in everything:
        copy.wait_send()


def finish(n_node, n_rep, ga, gb, cold, hot):
    sizes = sizes_of(n_node, n_rep)
    f32 = jnp.float32
    steps = sum(s - 1 for s in sizes.values())
    n_sems = 4 * steps + sizes["x"] - 1 + 1 + steps
    scratch = []
    for part, order in ((ga, ORDER_A), (gb, ORDER_B)):
        recv, acc = [], []
        for phase in range(4):
            rest = part.shape[phase + 1 :]
            recv.append(pltpu.VMEM((sizes[order[phase]] - 1, *rest), f32))
            acc.append(pltpu.VMEM(rest, f32))
        scratch += recv + acc
    scratch += [pltpu.SemaphoreType.DMA((n_sems,)), pltpu.SemaphoreType.DMA((n_sems,))]
    return pl.pallas_call(
        functools.partial(finish_kernel, n_node, n_rep, n_sems),
        out_shape=(
            jax.ShapeDtypeStruct(ga.shape, f32),
            jax.ShapeDtypeStruct(gb.shape, f32),
            jax.ShapeDtypeStruct((sizes["x"], 2, *cold.shape), f32),
            jax.ShapeDtypeStruct((*(sizes[a] for a in ORDER_A), *hot.shape), f32),
        ),
        in_specs=[VMEM] * 4,
        out_specs=(VMEM,) * 4,
        scratch_shapes=scratch,
        compiler_params=pltpu.CompilerParams(
            collective_id=1, has_side_effects=True, vmem_limit_bytes=40 * 1024 * 1024
        ),
    )(ga, gb, cold, hot)


def on_device(
    memory,
    hot_memory,
    cot_cold,
    cot_hot,
    src_local,
    dst_ids,
    times,
    edge_feat,
    cold_list,
    cold_count,
    hot_ids,
    time_freq,
    time_phase,
    w_msg,
    b_msg,
    w_in,
    w_hid,
):
    f32, bf16 = jnp.float32, jnp.bfloat16
    n_node = lax.axis_size("node")
    n_rep = lax.axis_size("rep")
    n_dev = n_node * n_rep
    rows_dev, width = memory.shape
    slot_cap = cold_list.shape[1]
    hot_rows = hot_memory.shape[0]
    events = src_local.shape[0]
    msg_width = w_msg.shape[1]
    band = hot_rows // n_dev
    share = rows_dev // n_rep
    rep = lax.axis_index("rep")
    me = lax.axis_index("node") * n_rep + rep
    hot_base = n_node * rows_dev

    pick = (src_local[:, None] == jnp.arange(rows_dev, dtype=jnp.int32)[None, :]).astype(bf16)
    src_mem = jnp.dot(pick, memory.astype(bf16), preferred_element_type=f32).astype(bf16)
    enc = jnp.cos(times.astype(f32)[:, None] * time_freq[None, :] + time_phase[None, :]).astype(bf16)
    raw = jnp.concatenate([src_mem, edge_feat, enc], axis=1)
    messages = jax.nn.silu(jnp.dot(raw, w_msg, preferred_element_type=f32) + b_msg[None, :]).astype(bf16)

    local_row = lax.rem(dst_ids, rows_dev)
    lane = jnp.arange(128, dtype=jnp.int32)[None, :]
    extra = jnp.where(
        lane == 0,
        1,
        jnp.where(
            lane == 1,
            lax.div(local_row, 32)[:, None],
            jnp.where(lane == 2, lax.rem(local_row, 32)[:, None], 0),
        ),
    ).astype(bf16)
    wide = jnp.concatenate([messages, extra], axis=1)
    hot_place = jnp.where(
        dst_ids >= hot_base, lax.rem(dst_ids - hot_base + hot_rows - me * band, hot_rows), -1
    )
    flat_list = cold_list.reshape(-1)
    event = jnp.arange(events, dtype=jnp.int32)[None, :]
    listed = (flat_list[:, None] == event).astype(bf16)
    hot_match = (jnp.arange(BANDS * band, dtype=jnp.int32)[:, None] == hot_place[None, :]).astype(bf16)
    sent = jnp.dot(listed, wide, preferred_element_type=f32)
    hot_part = jnp.dot(hot_match, wide, preferred_element_type=f32)
    send_msg = sent[:, :msg_width].astype(bf16).reshape(n_node, slot_cap, msg_width)
    slots = jnp.arange(slot_cap, dtype=jnp.int32)
    valid = slots[None, :] < cold_count[:, None]
    row_at = (sent[:, msg_width + 1] * 32.0 + sent[:, msg_width + 2]).astype(jnp.int32)
    send_row = jnp.where(valid, row_at.reshape(n_node, slot_cap), -1)
    send_row = jnp.pad(send_row, ((0, 0), (0, 128 - slot_cap)), constant_values=-1)
    send_row = jnp.broadcast_to(send_row[:, None, :], (n_node, 8, 128))

    cold_total, cold_cnt, hot_sum = exchange(
        n_node, n_rep, rows_dev, send_msg, send_row, hot_part.reshape(BANDS, band, msg_width + 128)
    )
    first = rep * share
    cold_number = lax.dynamic_index_in_dim(cold_cnt, rep, 0, keepdims=False)[0]
    total = jnp.concatenate([cold_total, hot_sum[:, :msg_width]], axis=0)
    count = jnp.concatenate([cold_number, hot_sum[:, msg_width]], axis=0)

    own_ids = hot_base + me * band + jnp.arange(band, dtype=jnp.int32)
    own = (own_ids[:, None] == hot_ids[None, :]).astype(f32)
    hot_state = jnp.dot(
        own, jnp.concatenate([hot_memory, cot_hot], axis=1), precision=lax.Precision.HIGHEST
    )
    mem = jnp.concatenate([lax.dynamic_slice_in_dim(memory, first, share, 0), hot_state[:, :width]], axis=0)
    cot = jnp.concatenate([lax.dynamic_slice_in_dim(cot_cold, first, share, 0), hot_state[:, width:]], axis=0)

    agg = (total / jnp.maximum(count, 1.0)[:, None]).astype(bf16)
    live = (count > 0)[:, None]
    gate_in = jnp.dot(agg, w_in, preferred_element_type=f32)
    mem_round = mem.astype(bf16)
    gate_hid = jnp.dot(mem_round, w_hid, preferred_element_type=f32)
    reset = jax.nn.sigmoid(gate_in[:, :width] + gate_hid[:, :width])
    update = jax.nn.sigmoid(gate_in[:, width : 2 * width] + gate_hid[:, width : 2 * width])
    hid_cand = gate_hid[:, 2 * width :]
    cand = jnp.tanh(gate_in[:, 2 * width :] + reset * hid_cand)
    fresh = jnp.where(live, (1.0 - update) * cand + update * mem, mem)
    cot = jnp.where(live, cot, 0.0)
    d_cand = cot * (1.0 - update) * (1.0 - cand * cand)
    d_upd = cot * (mem - cand) * update * (1.0 - update)
    d_reset = d_cand * hid_cand * reset * (1.0 - reset)
    d_input = jnp.concatenate([d_reset, d_upd, d_cand], axis=1) * GRAD_SCALE
    d_hidden = jnp.concatenate([d_reset, d_upd, d_cand * reset], axis=1) * GRAD_SCALE
    mem_wide = lax.optimization_barrier(mem_round).astype(f32)
    grad_a = jnp.dot(agg.astype(f32).T, d_input, precision=lax.Precision.HIGHEST)
    grad_b = jnp.dot(mem_wide.T, d_hidden, precision=lax.Precision.HIGHEST)
    grads = jnp.concatenate([grad_a, grad_b], axis=0)
    g_rows, g_cols = grads.shape
    half = g_cols // 2
    sizes = sizes_of(n_node, n_rep)
    piece = g_rows // n_dev
    ga = grads[:, :half].reshape(*(sizes[a] for a in ORDER_A), piece, half)
    gb = grads[:, half:].reshape(*(sizes[a] for a in ORDER_B), piece, half)
    oa, ob, new_cold, hot_blocks = finish(n_node, n_rep, ga, gb, fresh[:share], fresh[share:])
    grads = jnp.concatenate([oa.reshape(g_rows, half), ob.reshape(g_rows, half)], axis=1)
    agg_rows = w_in.shape[0]

    ids = hot_ids - hot_base
    block, inner = lax.div(ids, band), lax.rem(ids, band)
    at_node, at_rep = lax.div(block, n_rep), lax.rem(block, n_rep)
    hi, lo = lax.div(at_node, sizes["lo"]), lax.rem(at_node, sizes["lo"])
    xi, core = lax.div(at_rep, 2), lax.rem(at_rep, 2)
    place = (((core * sizes["x"] + xi) * sizes["lo"] + lo) * sizes["hi"] + hi) * band + inner
    new_hot = jnp.take(hot_blocks.reshape(hot_rows, width), place, axis=0)
    return (new_cold.reshape(rows_dev, width), new_hot, grads[:agg_rows], grads[agg_rows:])


def solution(mesh):
    both = P(("node", "rep"))
    in_specs = (
        P("node", None),
        P(),
        P("node", None),
        P(),
        both,
        both,
        both,
        P(("node", "rep"), None),
        P(("node", "rep"), None),
        both,
        P(),
        P(),
        P(),
        P(),
        P(),
        P(),
        P(),
    )
    out_specs = (P("node", None), P(), P(), P())
    return jax.shard_map(on_device, mesh=mesh, in_specs=in_specs, out_specs=out_specs, check_vma=False)
```

```python
import functools

import jax
import jax.numpy as jnp
from jax import lax
from jax.experimental import pallas as pl
from jax.experimental.pallas import tpu as pltpu
from jax.sharding import PartitionSpec as P

GRAD_SCALE = 1.0 / 64.0
BANDS = 4
MESH = pl.DeviceIdType.MESH
VMEM = pl.BlockSpec(memory_space=pltpu.VMEM)


def greet(devices):
    barrier = pltpu.get_barrier_semaphore()
    for device in devices:
        pl.semaphore_signal(barrier, inc=1, device_id=device, device_id_type=MESH)
    pl.semaphore_wait(barrier, len(devices))


def push(src, dst, send_sem, recv_sem, device):
    copy = pltpu.make_async_remote_copy(
        src_ref=src, dst_ref=dst, send_sem=send_sem, recv_sem=recv_sem, device_id=device, device_id_type=MESH
    )
    copy.start()
    return copy


def exchange_kernel(
    n_node, n_rep,
    msg0_ref, msg1_ref, rows_ref, hot_ref,
    sum_out, cnt_out, hot_out,
    recv0, recv1, rows_recv, hot_recv, sums, cnts, core_recv, x_send, x_recv, cnt_core, cnt_send, cnt_x,
    msg_s, msg_r, row_s, row_r, hot_s, hot_r, core_s, core_r, x_s, x_r, cc_s, cc_r, cx_s, cx_r,
):
    nx = n_rep // 2
    n_dev = n_node * n_rep
    node = lax.axis_index("node")
    rep = lax.axis_index("rep")
    core = lax.rem(rep, 2)
    xi = lax.div(rep, 2)
    me = node * n_rep + rep
    cap, part = msg0_ref.shape[1:]
    share = sum_out.shape[0]

    def at_node(k):
        return (lax.rem(node + k, n_node), rep)

    def at_linear(k):
        other = lax.rem(me + k, n_dev)
        return (lax.div(other, n_rep), lax.rem(other, n_rep))

    other_core = (node, xi * 2 + 1 - core)

    def at_x(k):
        return (node, lax.rem(xi + k, nx) * 2 + core)

    greet(
        [at_node(k) for k in range(1, n_node)]
        + [other_core]
        + [at_x(k) for k in range(1, nx)]
        + [at_linear(j) for j in range(1, BANDS)]
        + [at_linear(n_dev - j) for j in range(1, BANDS)]
    )

    sent = []
    arrivals = {}
    for k in range(1, n_node):
        other = lax.rem(node + k, n_node)
        arrivals["row", k] = push(rows_ref.at[other], rows_recv.at[node], row_s.at[k], row_r.at[k], at_node(k))
    for h, (src, dst) in enumerate(((msg0_ref, recv0), (msg1_ref, recv1))):
        for k in range(1, n_node):
            other = lax.rem(node + k, n_node)
            arrivals[h, k] = push(src.at[other], dst.at[node], msg_s.at[h, k], msg_r.at[h, k], at_node(k))
    sent += list(arrivals.values())
    hots = [
        push(hot_ref.at[j], hot_recv.at[j - 1], hot_s.at[j - 1], hot_r.at[j - 1], at_linear(j))
        for j in range(1, BANDS)
    ]
    sent += hots

    sums[...] = jnp.zeros_like(sums)
    cnts[...] = jnp.zeros_like(cnts)
    ones = jnp.ones((8, cap), jnp.bfloat16)

    def add_block(h, rows, block):
        for s in range(n_rep):
            spot = lax.broadcasted_iota(jnp.int32, (share, cap), 0) + s * share
            equal = jnp.where(spot == rows, 1.0, 0.0).astype(jnp.bfloat16)
            sums[h, s // 2, s % 2] += jnp.dot(equal, block, preferred_element_type=jnp.float32)
            if h == 0:
                cnts[s] += lax.dot_general(
                    ones, equal, (((1,), (1,)), ((), ())), preferred_element_type=jnp.float32
                )

    crossing = [[], []]
    counts = []
    for h, (mine, got) in enumerate(((msg0_ref, recv0), (msg1_ref, recv1))):
        add_block(h, rows_ref[node, 0:1, :cap], mine[node])
        for k in range(1, n_node):
            if h == 0:
                arrivals["row", k].wait_recv()
            arrivals[h, k].wait_recv()
            origin = lax.rem(node + n_node - k, n_node)
            add_block(h, rows_recv[origin, 0:1, :cap], got[origin])
        halves = []
        for k in [*range(1, nx), 0]:
            p = lax.rem(xi + k, nx)
            copy = push(sums.at[h, p, 1 - core], core_recv.at[h, k], core_s.at[h, k], core_r.at[h, k], other_core)
            halves.append((k, p, copy))
        if h == 0:
            cnt_copy = push(cnts, cnt_core, cc_s, cc_r, other_core)
            sent.append(cnt_copy)
        for k, p, copy in halves:
            copy.wait_recv()
            sent.append(copy)
            if k:
                x_send[h, k - 1] = sums[h, p, core] + core_recv[h, k]
                crossing[h].append(
                    push(x_send.at[h, k - 1], x_recv.at[h, k - 1], x_s.at[h, k - 1], x_r.at[h, k - 1], at_x(k))
                )
        if h == 0:
            cnt_copy.wait_recv()
            cnt_send[...] = cnts[...] + cnt_core[...]
            counts = [
                push(cnt_send, cnt_x.at[k - 1], cx_s.at[k - 1], cx_r.at[k - 1], at_x(k)) for k in range(1, nx)
            ]
    for copy in hots:
        copy.wait_recv()
    hot_out[...] = hot_ref[0] + hot_recv[0] + hot_recv[1] + hot_recv[2]
    number = cnt_send[...]
    for k, copy in enumerate(counts):
        copy.wait_recv()
        number += cnt_x[k]
    cnt_out[...] = number
    for h in range(2):
        total = sums[h, xi, core] + core_recv[h, 0]
        for k, copy in enumerate(crossing[h]):
            copy.wait_recv()
            total += x_recv[h, k]
        sum_out[:, h * part : (h + 1) * part] = total
    for copy in [*sent, *crossing[0], *crossing[1], *counts]:
        copy.wait_send()


def exchange(n_node, n_rep, rows_dev, msg0, msg1, rows, hot):
    nx = n_rep // 2
    part = msg0.shape[2]
    band, hot_width = hot.shape[1:]
    share = rows_dev // n_rep
    dma = pltpu.SemaphoreType.DMA
    f32 = jnp.float32
    return pl.pallas_call(
        functools.partial(exchange_kernel, n_node, n_rep),
        out_shape=(
            jax.ShapeDtypeStruct((share, 2 * part), f32),
            jax.ShapeDtypeStruct((n_rep, 8, share), f32),
            jax.ShapeDtypeStruct((band, hot_width), f32),
        ),
        in_specs=[VMEM] * 4,
        out_specs=(VMEM,) * 3,
        scratch_shapes=[
            pltpu.VMEM(msg0.shape, msg0.dtype),
            pltpu.VMEM(msg1.shape, msg1.dtype),
            pltpu.VMEM(rows.shape, rows.dtype),
            pltpu.VMEM((BANDS - 1, band, hot_width), f32),
            pltpu.VMEM((2, nx, 2, share, part), f32),
            pltpu.VMEM((n_rep, 8, share), f32),
            pltpu.VMEM((2, nx, share, part), f32),
            pltpu.VMEM((2, nx - 1, share, part), f32),
            pltpu.VMEM((2, nx - 1, share, part), f32),
            pltpu.VMEM((n_rep, 8, share), f32),
            pltpu.VMEM((n_rep, 8, share), f32),
            pltpu.VMEM((nx - 1, n_rep, 8, share), f32),
            dma((2, n_node)), dma((2, n_node)), dma((n_node,)), dma((n_node,)),
            dma((BANDS - 1,)), dma((BANDS - 1,)),
            dma((2, nx)), dma((2, nx)),
            dma((2, nx - 1)), dma((2, nx - 1)),
            dma, dma,
            dma((nx - 1,)), dma((nx - 1,)),
        ],
        compiler_params=pltpu.CompilerParams(
            collective_id=0, has_side_effects=True, vmem_limit_bytes=40 * 1024 * 1024
        ),
    )(msg0, msg1, rows, hot)


ORDER_A = ("core", "x", "lo", "hi")
ORDER_B = ("core", "lo", "x", "hi")


def sizes_of(n_node, n_rep):
    return {"core": 2, "x": n_rep // 2, "lo": n_node // 4, "hi": 4}


def finish_kernel(n_node, n_rep, ga_ref, gb_ref, cold_ref, hot_ref, place_ref, oa, ob, ocold, new_hot, *scratch):
    sizes = sizes_of(n_node, n_rep)
    recv_a, acc_a, recv_b, acc_b = scratch[0:4], scratch[4:8], scratch[8:12], scratch[12:16]
    send_sem, recv_sem = scratch[16:18]
    band, width = hot_ref.shape
    tidy = band % 8 == 0
    ohot, pieces = scratch[18:20] if tidy else (new_hot, None)
    node = lax.axis_index("node")
    rep = lax.axis_index("rep")
    nlo = sizes["lo"]
    mine = {"core": lax.rem(rep, 2), "x": lax.div(rep, 2), "lo": lax.rem(node, nlo), "hi": lax.div(node, nlo)}

    def peer(axis, k):
        spot = dict(mine)
        spot[axis] = lax.rem(mine[axis] + k, sizes[axis])
        return (spot["hi"] * nlo + spot["lo"], spot["x"] * 2 + spot["core"])

    greet([peer(axis, k) for axis in ORDER_A for k in range(1, sizes[axis])])

    used = [0]
    everything = []

    def ship(src, dst, device):
        i = used[0]
        used[0] += 1
        copy = push(src, dst, send_sem.at[i], recv_sem.at[i], device)
        everything.append(copy)
        return copy

    def scatter_start(cur, recv, axis):
        size = sizes[axis]
        return [
            ship(cur.at[lax.rem(mine[axis] + k, size)], recv.at[k - 1], peer(axis, k)) for k in range(1, size)
        ]

    def scatter_end(copies, cur, recv, acc, axis):
        total = cur[mine[axis]]
        for k, copy in enumerate(copies):
            copy.wait_recv()
            total = total + recv[k]
        acc[...] = total

    def gather_start(out, order, phase):
        axis = order[phase]
        where = out.at[tuple(mine[a] for a in order[: phase + 1])]
        return [ship(where, where, peer(axis, k)) for k in range(1, sizes[axis])]

    def arrive(copies):
        for copy in copies:
            copy.wait_recv()

    ocold[mine["x"], mine["core"]] = cold_ref[...]
    ohot[tuple(mine[a] for a in ORDER_A)] = hot_ref[...]
    cold_place = ocold.at[mine["x"], mine["core"]]
    first_a = scatter_start(ga_ref, recv_a[0], ORDER_A[0])
    first_b = scatter_start(gb_ref, recv_b[0], ORDER_B[0])
    cold_copies = [ship(cold_place, cold_place, peer("x", k)) for k in range(1, sizes["x"])]
    hot_copies = gather_start(ohot, ORDER_A, 3)

    cur_a, cur_b, copies_a, copies_b = ga_ref, gb_ref, first_a, first_b
    for phase in range(4):
        scatter_end(copies_a, cur_a, recv_a[phase], acc_a[phase], ORDER_A[phase])
        cur_a = acc_a[phase]
        if phase < 3:
            copies_a = scatter_start(cur_a, recv_a[phase + 1], ORDER_A[phase + 1])
        scatter_end(copies_b, cur_b, recv_b[phase], acc_b[phase], ORDER_B[phase])
        cur_b = acc_b[phase]
        if phase < 3:
            copies_b = scatter_start(cur_b, recv_b[phase + 1], ORDER_B[phase + 1])
        if phase == 0:
            arrive(hot_copies)
            hot_copies = gather_start(ohot, ORDER_A, 2)
        if phase == 1:
            arrive(cold_copies)
            side = ocold.at[:, mine["core"]]
            cold_copies = [ship(side, side, peer("core", 1))]
        if phase == 2:
            arrive(hot_copies)
            hot_copies = gather_start(ohot, ORDER_A, 1)
        if phase == 3:
            arrive(hot_copies)
            hot_copies = gather_start(ohot, ORDER_A, 0)
    oa[tuple(mine[a] for a in ORDER_A)] = cur_a[...]
    ob[tuple(mine[a] for a in ORDER_B)] = cur_b[...]
    for phase in (3, 2, 1, 0):
        copies_a = gather_start(oa, ORDER_A, phase)
        copies_b = gather_start(ob, ORDER_B, phase)
        if phase == 2:
            arrive(hot_copies)
            if tidy:
                hot_rows = new_hot.shape[0]
                rows = ohot[...].reshape(hot_rows, width)
                top = rows.astype(jnp.bfloat16)
                rest = rows - top.astype(jnp.float32)
                middle = rest.astype(jnp.bfloat16)
                low = (rest - middle.astype(jnp.float32)).astype(jnp.bfloat16)
                pieces[:, :width] = top
                pieces[:, width : 2 * width] = middle
                pieces[:, 2 * width :] = low
                step = hot_rows // 4
                for part in range(4):
                    chosen = lax.broadcasted_iota(jnp.int32, (hot_rows, step), 0)
                    chosen = chosen == place_ref[0:1, part * step : (part + 1) * step]
                    got = lax.dot_general(
                        jnp.where(chosen, 1.0, 0.0).astype(jnp.bfloat16),
                        pieces[...],
                        (((0,), (0,)), ((), ())),
                        preferred_element_type=jnp.float32,
                    )
                    new_hot[part * step : (part + 1) * step] = (
                        got[:, :width] + got[:, width : 2 * width] + got[:, 2 * width :]
                    )
        arrive(copies_a)
        arrive(copies_b)
    arrive(cold_copies)
    for copy in everything:
        copy.wait_send()


def finish(n_node, n_rep, ga, gb, cold, hot, place):
    sizes = sizes_of(n_node, n_rep)
    f32 = jnp.float32
    steps = sum(s - 1 for s in sizes.values())
    n_sems = 4 * steps + sizes["x"] - 1 + 1 + steps
    scratch = []
    for part, order in ((ga, ORDER_A), (gb, ORDER_B)):
        recv, acc = [], []
        for phase in range(4):
            rest = part.shape[phase + 1 :]
            recv.append(pltpu.VMEM((sizes[order[phase]] - 1, *rest), f32))
            acc.append(pltpu.VMEM(rest, f32))
        scratch += recv + acc
    scratch += [pltpu.SemaphoreType.DMA((n_sems,)), pltpu.SemaphoreType.DMA((n_sems,))]
    blocks = (*(sizes[a] for a in ORDER_A), *hot.shape)
    band, width = hot.shape
    hot_rows = place.shape[1]
    out_hot = jax.ShapeDtypeStruct(blocks, f32)
    if band % 8 == 0:
        out_hot = jax.ShapeDtypeStruct((hot_rows, width), f32)
        scratch += [pltpu.VMEM(blocks, f32), pltpu.VMEM((hot_rows, 3 * width), jnp.bfloat16)]
    return pl.pallas_call(
        functools.partial(finish_kernel, n_node, n_rep),
        out_shape=(
            jax.ShapeDtypeStruct(ga.shape, f32),
            jax.ShapeDtypeStruct(gb.shape, f32),
            jax.ShapeDtypeStruct((sizes["x"], 2, *cold.shape), f32),
            out_hot,
        ),
        in_specs=[VMEM] * 5,
        out_specs=(VMEM,) * 4,
        scratch_shapes=scratch,
        compiler_params=pltpu.CompilerParams(
            collective_id=1, has_side_effects=True, vmem_limit_bytes=40 * 1024 * 1024
        ),
    )(ga, gb, cold, hot, place)


def on_device(
    memory,
    hot_memory,
    cot_cold,
    cot_hot,
    src_local,
    dst_ids,
    times,
    edge_feat,
    cold_list,
    cold_count,
    hot_ids,
    time_freq,
    time_phase,
    w_msg,
    b_msg,
    w_in,
    w_hid,
):
    f32, bf16 = jnp.float32, jnp.bfloat16
    n_node = lax.axis_size("node")
    n_rep = lax.axis_size("rep")
    n_dev = n_node * n_rep
    rows_dev, width = memory.shape
    slot_cap = cold_list.shape[1]
    hot_rows = hot_memory.shape[0]
    events = src_local.shape[0]
    msg_width = w_msg.shape[1]
    band = hot_rows // n_dev
    share = rows_dev // n_rep
    rep = lax.axis_index("rep")
    me = lax.axis_index("node") * n_rep + rep
    hot_base = n_node * rows_dev

    pick = (src_local[:, None] == jnp.arange(rows_dev, dtype=jnp.int32)[None, :]).astype(bf16)
    src_mem = jnp.dot(pick, memory.astype(bf16), preferred_element_type=f32).astype(bf16)
    enc = jnp.cos(times.astype(f32)[:, None] * time_freq[None, :] + time_phase[None, :]).astype(bf16)
    raw = jnp.concatenate([src_mem, edge_feat, enc], axis=1)
    messages = jax.nn.silu(jnp.dot(raw, w_msg, preferred_element_type=f32) + b_msg[None, :]).astype(bf16)

    local_row = lax.rem(dst_ids, rows_dev)
    lane = jnp.arange(128, dtype=jnp.int32)[None, :]
    extra = jnp.where(
        lane == 0, lax.div(local_row, 32)[:, None], jnp.where(lane == 1, lax.rem(local_row, 32)[:, None], 0)
    ).astype(bf16)
    hot_place = jnp.where(
        dst_ids >= hot_base, lax.rem(dst_ids - hot_base + hot_rows - me * band, hot_rows), -1
    )
    flat_list = cold_list.reshape(-1)
    event = jnp.arange(events, dtype=jnp.int32)[None, :]
    listed = (flat_list[:, None] == event).astype(bf16)
    hot_match = (jnp.arange(BANDS * band, dtype=jnp.int32)[:, None] == hot_place[None, :]).astype(bf16)
    part = msg_width // 2
    msg0, msg1 = (
        jnp.dot(listed, messages[:, h * part : (h + 1) * part], preferred_element_type=f32)
        .astype(bf16)
        .reshape(n_node, slot_cap, part)
        for h in range(2)
    )
    sent = jnp.dot(listed, extra, preferred_element_type=f32)
    hot_part = jnp.dot(hot_match, messages, preferred_element_type=f32)
    hot_number = jnp.sum(hot_match.astype(f32), axis=1)
    hot_part = jnp.concatenate(
        [hot_part, jnp.broadcast_to(hot_number[:, None], (BANDS * band, 128))], axis=1
    )
    slots = jnp.arange(slot_cap, dtype=jnp.int32)
    valid = slots[None, :] < cold_count[:, None]
    row_at = (sent[:, 0] * 32.0 + sent[:, 1]).astype(jnp.int32)
    send_row = jnp.where(valid, row_at.reshape(n_node, slot_cap), -1)
    send_row = jnp.pad(send_row, ((0, 0), (0, 128 - slot_cap)), constant_values=-1)
    send_row = jnp.broadcast_to(send_row[:, None, :], (n_node, 8, 128))

    cold_total, cold_cnt, hot_sum = exchange(
        n_node, n_rep, rows_dev, msg0, msg1, send_row, hot_part.reshape(BANDS, band, msg_width + 128)
    )
    first = rep * share
    cold_number = lax.dynamic_index_in_dim(cold_cnt, rep, 0, keepdims=False)[0]
    total = jnp.concatenate([cold_total, hot_sum[:, :msg_width]], axis=0)
    count = jnp.concatenate([cold_number, hot_sum[:, msg_width]], axis=0)

    own_ids = hot_base + me * band + jnp.arange(band, dtype=jnp.int32)
    own = (own_ids[:, None] == hot_ids[None, :]).astype(f32)
    hot_state = jnp.dot(
        own, jnp.concatenate([hot_memory, cot_hot], axis=1), precision=lax.Precision.HIGHEST
    )
    mem = jnp.concatenate([lax.dynamic_slice_in_dim(memory, first, share, 0), hot_state[:, :width]], axis=0)
    cot = jnp.concatenate([lax.dynamic_slice_in_dim(cot_cold, first, share, 0), hot_state[:, width:]], axis=0)

    agg = (total / jnp.maximum(count, 1.0)[:, None]).astype(bf16)
    live = (count > 0)[:, None]
    gate_in = jnp.dot(agg, w_in, preferred_element_type=f32)
    mem_round = mem.astype(bf16)
    gate_hid = jnp.dot(mem_round, w_hid, preferred_element_type=f32)
    reset = jax.nn.sigmoid(gate_in[:, :width] + gate_hid[:, :width])
    update = jax.nn.sigmoid(gate_in[:, width : 2 * width] + gate_hid[:, width : 2 * width])
    hid_cand = gate_hid[:, 2 * width :]
    cand = jnp.tanh(gate_in[:, 2 * width :] + reset * hid_cand)
    fresh = jnp.where(live, (1.0 - update) * cand + update * mem, mem)
    cot = jnp.where(live, cot, 0.0)
    d_cand = cot * (1.0 - update) * (1.0 - cand * cand)
    d_upd = cot * (mem - cand) * update * (1.0 - update)
    d_reset = d_cand * hid_cand * reset * (1.0 - reset)
    d_input = jnp.concatenate([d_reset, d_upd, d_cand], axis=1) * GRAD_SCALE
    d_hidden = jnp.concatenate([d_reset, d_upd, d_cand * reset], axis=1) * GRAD_SCALE
    mem_wide = lax.optimization_barrier(mem_round).astype(f32)
    grad_a = jnp.dot(agg.astype(f32).T, d_input, precision=lax.Precision.HIGHEST)
    grad_b = jnp.dot(mem_wide.T, d_hidden, precision=lax.Precision.HIGHEST)
    grads = jnp.concatenate([grad_a, grad_b], axis=0)
    g_rows, g_cols = grads.shape
    half = g_cols // 2
    sizes = sizes_of(n_node, n_rep)
    piece = g_rows // n_dev
    ga = grads[:, :half].reshape(*(sizes[a] for a in ORDER_A), piece, half)
    gb = grads[:, half:].reshape(*(sizes[a] for a in ORDER_B), piece, half)
    ids = hot_ids - hot_base
    block, inner = lax.div(ids, band), lax.rem(ids, band)
    at_node, at_rep = lax.div(block, n_rep), lax.rem(block, n_rep)
    hi, lo = lax.div(at_node, sizes["lo"]), lax.rem(at_node, sizes["lo"])
    xi, core = lax.div(at_rep, 2), lax.rem(at_rep, 2)
    place = (((core * sizes["x"] + xi) * sizes["lo"] + lo) * sizes["hi"] + hi) * band + inner
    place_rows = jnp.broadcast_to(place[None, :], (8, hot_rows))
    oa, ob, new_cold, new_hot = finish(n_node, n_rep, ga, gb, fresh[:share], fresh[share:], place_rows)
    grads = jnp.concatenate([oa.reshape(g_rows, half), ob.reshape(g_rows, half)], axis=1)
    agg_rows = w_in.shape[0]

    if band % 8:
        new_hot = jnp.take(new_hot.reshape(hot_rows, width), place, axis=0)
    return (new_cold.reshape(rows_dev, width), new_hot, grads[:agg_rows], grads[agg_rows:])


def solution(mesh):
    both = P(("node", "rep"))
    in_specs = (
        P("node", None),
        P(),
        P("node", None),
        P(),
        both,
        both,
        both,
        P(("node", "rep"), None),
        P(("node", "rep"), None),
        both,
        P(),
        P(),
        P(),
        P(),
        P(),
        P(),
        P(),
    )
    out_specs = (P("node", None), P(), P(), P())
    return jax.shard_map(on_device, mesh=mesh, in_specs=in_specs, out_specs=out_specs, check_vma=False)
```

```python
import functools
import math

import jax
import jax.numpy as jnp
from jax import lax
from jax.experimental import pallas as pl
from jax.experimental.pallas import tpu as pltpu
from jax.sharding import PartitionSpec as P

GRAD_SCALE = 1.0 / 64.0
BANDS = 4
MESH = pl.DeviceIdType.MESH
VMEM = pl.BlockSpec(memory_space=pltpu.VMEM)


def greet(devices):
    barrier = pltpu.get_barrier_semaphore()
    for device in devices:
        pl.semaphore_signal(barrier, inc=1, device_id=device, device_id_type=MESH)
    pl.semaphore_wait(barrier, len(devices))


def push(src, dst, send_sem, recv_sem, device):
    copy = pltpu.make_async_remote_copy(
        src_ref=src, dst_ref=dst, send_sem=send_sem, recv_sem=recv_sem, device_id=device, device_id_type=MESH
    )
    copy.start()
    return copy


def exchange_kernel(
    n_node, n_rep,
    msg0_ref, msg1_ref, rows_ref, hot_ref,
    sum_out, cnt_out, hot_out,
    recv0, recv1, rows_recv, hot_recv, sums, cnts, core_recv, x_send, x_recv, cnt_core, cnt_send, cnt_x,
    msg_s, msg_r, row_s, row_r, hot_s, hot_r, core_s, core_r, x_s, x_r, cc_s, cc_r, cx_s, cx_r,
):
    nx = n_rep // 2
    n_dev = n_node * n_rep
    node = lax.axis_index("node")
    rep = lax.axis_index("rep")
    core = lax.rem(rep, 2)
    xi = lax.div(rep, 2)
    me = node * n_rep + rep
    cap, part = msg0_ref.shape[1:]
    share = sum_out.shape[0]

    def at_node(k):
        return (lax.rem(node + k, n_node), rep)

    def at_linear(k):
        other = lax.rem(me + k, n_dev)
        return (lax.div(other, n_rep), lax.rem(other, n_rep))

    other_core = (node, xi * 2 + 1 - core)

    def at_x(k):
        return (node, lax.rem(xi + k, nx) * 2 + core)

    greet(
        [at_node(k) for k in range(1, n_node)]
        + [other_core]
        + [at_x(k) for k in range(1, nx)]
        + [at_linear(j) for j in range(1, BANDS)]
        + [at_linear(n_dev - j) for j in range(1, BANDS)]
    )

    sent = []
    arrivals = {}
    for k in range(1, n_node):
        other = lax.rem(node + k, n_node)
        arrivals["row", k] = push(rows_ref.at[other], rows_recv.at[node], row_s.at[k], row_r.at[k], at_node(k))
    for h, (src, dst) in enumerate(((msg0_ref, recv0), (msg1_ref, recv1))):
        for k in range(1, n_node):
            other = lax.rem(node + k, n_node)
            arrivals[h, k] = push(src.at[other], dst.at[node], msg_s.at[h, k], msg_r.at[h, k], at_node(k))
    sent += list(arrivals.values())
    hots = [
        push(hot_ref.at[j], hot_recv.at[j - 1], hot_s.at[j - 1], hot_r.at[j - 1], at_linear(j))
        for j in range(1, BANDS)
    ]
    sent += hots

    sums[...] = jnp.zeros_like(sums)
    cnts[...] = jnp.zeros_like(cnts)
    ones = jnp.ones((8, cap), jnp.bfloat16)

    def add_block(h, rows, block):
        for s in range(n_rep):
            spot = lax.broadcasted_iota(jnp.int32, (share, cap), 0) + s * share
            equal = jnp.where(spot == rows, 1.0, 0.0).astype(jnp.bfloat16)
            sums[h, s // 2, s % 2] += jnp.dot(equal, block, preferred_element_type=jnp.float32)
            if h == 0:
                cnts[s] += lax.dot_general(
                    ones, equal, (((1,), (1,)), ((), ())), preferred_element_type=jnp.float32
                )

    crossing = [[], []]
    counts = []
    for h, (mine, got) in enumerate(((msg0_ref, recv0), (msg1_ref, recv1))):
        add_block(h, rows_ref[node, 0:1, :cap], mine[node])
        for k in range(1, n_node):
            if h == 0:
                arrivals["row", k].wait_recv()
            arrivals[h, k].wait_recv()
            origin = lax.rem(node + n_node - k, n_node)
            add_block(h, rows_recv[origin, 0:1, :cap], got[origin])
        halves = []
        for k in [*range(1, nx), 0]:
            p = lax.rem(xi + k, nx)
            copy = push(sums.at[h, p, 1 - core], core_recv.at[h, k], core_s.at[h, k], core_r.at[h, k], other_core)
            halves.append((k, p, copy))
        if h == 0:
            cnt_copy = push(cnts, cnt_core, cc_s, cc_r, other_core)
            sent.append(cnt_copy)
        for k, p, copy in halves:
            copy.wait_recv()
            sent.append(copy)
            if k:
                x_send[h, k - 1] = sums[h, p, core] + core_recv[h, k]
                crossing[h].append(
                    push(x_send.at[h, k - 1], x_recv.at[h, k - 1], x_s.at[h, k - 1], x_r.at[h, k - 1], at_x(k))
                )
        if h == 0:
            cnt_copy.wait_recv()
            cnt_send[...] = cnts[...] + cnt_core[...]
            counts = [
                push(cnt_send, cnt_x.at[k - 1], cx_s.at[k - 1], cx_r.at[k - 1], at_x(k)) for k in range(1, nx)
            ]
    for copy in hots:
        copy.wait_recv()
    hot_out[...] = hot_ref[0] + hot_recv[0] + hot_recv[1] + hot_recv[2]
    number = cnt_send[...]
    for k, copy in enumerate(counts):
        copy.wait_recv()
        number += cnt_x[k]
    cnt_out[...] = number
    for h in range(2):
        total = sums[h, xi, core] + core_recv[h, 0]
        for k, copy in enumerate(crossing[h]):
            copy.wait_recv()
            total += x_recv[h, k]
        sum_out[:, h * part : (h + 1) * part] = total
    for copy in [*sent, *crossing[0], *crossing[1], *counts]:
        copy.wait_send()


def exchange(n_node, n_rep, rows_dev, msg0, msg1, rows, hot):
    nx = n_rep // 2
    part = msg0.shape[2]
    band, hot_width = hot.shape[1:]
    share = rows_dev // n_rep
    dma = pltpu.SemaphoreType.DMA
    f32 = jnp.float32
    return pl.pallas_call(
        functools.partial(exchange_kernel, n_node, n_rep),
        out_shape=(
            jax.ShapeDtypeStruct((share, 2 * part), f32),
            jax.ShapeDtypeStruct((n_rep, 8, share), f32),
            jax.ShapeDtypeStruct((band, hot_width), f32),
        ),
        in_specs=[VMEM] * 4,
        out_specs=(VMEM,) * 3,
        scratch_shapes=[
            pltpu.VMEM(msg0.shape, msg0.dtype),
            pltpu.VMEM(msg1.shape, msg1.dtype),
            pltpu.VMEM(rows.shape, rows.dtype),
            pltpu.VMEM((BANDS - 1, band, hot_width), f32),
            pltpu.VMEM((2, nx, 2, share, part), f32),
            pltpu.VMEM((n_rep, 8, share), f32),
            pltpu.VMEM((2, nx, share, part), f32),
            pltpu.VMEM((2, nx - 1, share, part), f32),
            pltpu.VMEM((2, nx - 1, share, part), f32),
            pltpu.VMEM((n_rep, 8, share), f32),
            pltpu.VMEM((n_rep, 8, share), f32),
            pltpu.VMEM((nx - 1, n_rep, 8, share), f32),
            dma((2, n_node)), dma((2, n_node)), dma((n_node,)), dma((n_node,)),
            dma((BANDS - 1,)), dma((BANDS - 1,)),
            dma((2, nx)), dma((2, nx)),
            dma((2, nx - 1)), dma((2, nx - 1)),
            dma, dma,
            dma((nx - 1,)), dma((nx - 1,)),
        ],
        compiler_params=pltpu.CompilerParams(
            collective_id=0, has_side_effects=True, vmem_limit_bytes=40 * 1024 * 1024
        ),
    )(msg0, msg1, rows, hot)


ORDER_A = ("core", "x", "lo", "hi")
ORDER_B = ("core", "lo", "x", "hi")
ORDER_HOT = ("core", "lo", "hi", "x")
LANES = 128


def sizes_of(n_node, n_rep):
    return {"core": 2, "x": n_rep // 2, "lo": n_node // 4, "hi": 4}


def span(sizes, order, phase):
    return math.prod(sizes[a] for a in order[phase + 1 :])


def parts_of(columns):
    return [(first, ORDER_B if i % 2 else ORDER_A) for i, first in enumerate(range(0, columns, LANES))]


def finish_kernel(n_node, n_rep, g_ref, cold_ref, hot_ref, place_ref, og, ocold, new_hot, *scratch):
    sizes = sizes_of(n_node, n_rep)
    parts = parts_of(g_ref.shape[2])
    send_sem, recv_sem = scratch[:2]
    buffers = scratch[2 : 2 + 8 * len(parts)]
    band, width = hot_ref.shape
    tidy = band % 8 == 0
    ohot, pieces = scratch[2 + 8 * len(parts) :] if tidy else (new_hot, None)
    node = lax.axis_index("node")
    rep = lax.axis_index("rep")
    nlo = sizes["lo"]
    mine = {"core": lax.rem(rep, 2), "x": lax.div(rep, 2), "lo": lax.rem(node, nlo), "hi": lax.div(node, nlo)}

    def peer(axis, k):
        spot = dict(mine)
        spot[axis] = lax.rem(mine[axis] + k, sizes[axis])
        return (spot["hi"] * nlo + spot["lo"], spot["x"] * 2 + spot["core"])

    greet([peer(axis, k) for axis in ORDER_A for k in range(1, sizes[axis])])

    everything = []

    def ship(src, dst, device):
        i = len(everything)
        copy = push(src, dst, send_sem.at[i], recv_sem.at[i], device)
        everything.append(copy)
        return copy

    def arrive(copies):
        for copy in copies:
            copy.wait_recv()

    def held(part, phase):
        first, order = parts[part]
        if phase == 0:
            return lambda i, n: g_ref.at[pl.ds(i, n), :, pl.ds(first, LANES)]
        acc = buffers[8 * part + 2 * (phase - 1) + 1]
        return lambda i, n: acc.at[pl.ds(i, n)]

    def scatter_start(part, phase):
        order = parts[part][1]
        axis = order[phase]
        size, n = sizes[axis], span(sizes, order, phase)
        view, recv = held(part, phase), buffers[8 * part + 2 * phase]
        return [
            ship(view(lax.rem(mine[axis] + k, size) * n, n), recv.at[k - 1], peer(axis, k)) for k in range(1, size)
        ]

    def scatter_end(part, phase, copies):
        order = parts[part][1]
        axis = order[phase]
        n = span(sizes, order, phase)
        recv, acc = buffers[8 * part + 2 * phase], buffers[8 * part + 2 * phase + 1]
        total = held(part, phase)(mine[axis] * n, n)[...]
        for k, copy in enumerate(copies):
            copy.wait_recv()
            total = total + recv[k]
        acc[...] = total

    def prefix(order, phase):
        return sum(mine[order[i]] * span(sizes, order, i) for i in range(phase + 1))

    def gather_start(part, phase):
        first, order = parts[part]
        axis = order[phase]
        where = og.at[pl.ds(prefix(order, phase), span(sizes, order, phase)), :, pl.ds(first, LANES)]
        return [ship(where, where, peer(axis, k)) for k in range(1, sizes[axis])]

    def hot_start(phase):
        axis = ORDER_HOT[phase]
        where = ohot.at[pl.ds(prefix(ORDER_HOT, phase), span(sizes, ORDER_HOT, phase))]
        return [ship(where, where, peer(axis, k)) for k in range(1, sizes[axis])]

    everyone = range(len(parts))
    flying = [scatter_start(part, 0) for part in everyone]
    ocold[mine["x"], mine["core"]] = cold_ref[...]
    ohot[prefix(ORDER_HOT, 3)] = hot_ref[...]
    cold_place = ocold.at[mine["x"], mine["core"]]
    hot_copies = hot_start(3)
    cold_copies = [ship(cold_place, cold_place, peer("x", k)) for k in range(1, sizes["x"])]

    for phase in range(4):
        for part in everyone:
            scatter_end(part, phase, flying[part])
            if phase < 3:
                flying[part] = scatter_start(part, phase + 1)
            else:
                first, order = parts[part]
                og[pl.ds(prefix(order, 3), 1), :, first : first + LANES] = buffers[8 * part + 7][...]
                flying[part] = gather_start(part, 3)
        arrive(hot_copies)
        hot_copies = hot_start(2 - phase) if phase < 3 else []
        if phase == 1:
            arrive(cold_copies)
            side = ocold.at[:, mine["core"]]
            cold_copies = [ship(side, side, peer("core", 1))]
    if tidy:
        hot_rows = new_hot.shape[0]
        rows = ohot[...].reshape(hot_rows, width)
        top = rows.astype(jnp.bfloat16)
        rest = rows - top.astype(jnp.float32)
        middle = rest.astype(jnp.bfloat16)
        pieces[:, :width] = top
        pieces[:, width : 2 * width] = middle
        pieces[:, 2 * width :] = (rest - middle.astype(jnp.float32)).astype(jnp.bfloat16)

    def permute_hot(part):
        step = new_hot.shape[0] // 4
        chosen = lax.broadcasted_iota(jnp.int32, (new_hot.shape[0], step), 0)
        chosen = chosen == place_ref[0:1, part * step : (part + 1) * step]
        got = lax.dot_general(
            jnp.where(chosen, 1.0, 0.0).astype(jnp.bfloat16),
            pieces[...],
            (((0,), (0,)), ((), ())),
            preferred_element_type=jnp.float32,
        )
        new_hot[part * step : (part + 1) * step] = got[:, :width] + got[:, width : 2 * width] + got[:, 2 * width :]

    for phase in (3, 2, 1, 0):
        for part in everyone:
            arrive(flying[part])
            flying[part] = gather_start(part, phase - 1) if phase else []
        if tidy:
            permute_hot(3 - phase)
    arrive(cold_copies)
    for copy in everything:
        copy.wait_send()


def finish(n_node, n_rep, grads, cold, hot, place):
    sizes = sizes_of(n_node, n_rep)
    f32 = jnp.float32
    n_dev, piece, columns = grads.shape
    parts = parts_of(columns)
    steps = sum(s - 1 for s in sizes.values())
    n_sems = 2 * steps * len(parts) + steps + sizes["x"] - 1 + 1
    scratch = [pltpu.SemaphoreType.DMA((n_sems,)), pltpu.SemaphoreType.DMA((n_sems,))]
    for first, order in parts:
        for phase in range(4):
            block = (span(sizes, order, phase), piece, LANES)
            scratch += [pltpu.VMEM((sizes[order[phase]] - 1, *block), f32), pltpu.VMEM(block, f32)]
    band, width = hot.shape
    hot_rows = place.shape[1]
    blocks = (n_dev, band, width)
    out_hot = jax.ShapeDtypeStruct(blocks, f32)
    if band % 8 == 0:
        out_hot = jax.ShapeDtypeStruct((hot_rows, width), f32)
        scratch += [pltpu.VMEM(blocks, f32), pltpu.VMEM((hot_rows, 3 * width), jnp.bfloat16)]
    return pl.pallas_call(
        functools.partial(finish_kernel, n_node, n_rep),
        out_shape=(
            jax.ShapeDtypeStruct(grads.shape, f32),
            jax.ShapeDtypeStruct((sizes["x"], 2, *cold.shape), f32),
            out_hot,
        ),
        in_specs=[VMEM] * 4,
        out_specs=(VMEM,) * 3,
        scratch_shapes=scratch,
        compiler_params=pltpu.CompilerParams(
            collective_id=1, has_side_effects=True, vmem_limit_bytes=40 * 1024 * 1024
        ),
    )(grads, cold, hot, place)


def on_device(
    memory,
    hot_memory,
    cot_cold,
    cot_hot,
    src_local,
    dst_ids,
    times,
    edge_feat,
    cold_list,
    cold_count,
    hot_ids,
    time_freq,
    time_phase,
    w_msg,
    b_msg,
    w_in,
    w_hid,
):
    f32, bf16 = jnp.float32, jnp.bfloat16
    n_node = lax.axis_size("node")
    n_rep = lax.axis_size("rep")
    n_dev = n_node * n_rep
    rows_dev, width = memory.shape
    slot_cap = cold_list.shape[1]
    hot_rows = hot_memory.shape[0]
    events = src_local.shape[0]
    msg_width = w_msg.shape[1]
    band = hot_rows // n_dev
    share = rows_dev // n_rep
    rep = lax.axis_index("rep")
    me = lax.axis_index("node") * n_rep + rep
    hot_base = n_node * rows_dev

    pick = (src_local[:, None] == jnp.arange(rows_dev, dtype=jnp.int32)[None, :]).astype(bf16)
    src_mem = jnp.dot(pick, memory.astype(bf16), preferred_element_type=f32).astype(bf16)
    enc = jnp.cos(times.astype(f32)[:, None] * time_freq[None, :] + time_phase[None, :]).astype(bf16)
    raw = jnp.concatenate([src_mem, edge_feat, enc], axis=1)
    messages = jax.nn.silu(jnp.dot(raw, w_msg, preferred_element_type=f32) + b_msg[None, :]).astype(bf16)

    local_row = lax.rem(dst_ids, rows_dev)
    lane = jnp.arange(128, dtype=jnp.int32)[None, :]
    extra = jnp.where(
        lane == 0, lax.div(local_row, 32)[:, None], jnp.where(lane == 1, lax.rem(local_row, 32)[:, None], 0)
    ).astype(bf16)
    hot_place = jnp.where(
        dst_ids >= hot_base, lax.rem(dst_ids - hot_base + hot_rows - me * band, hot_rows), -1
    )
    flat_list = cold_list.reshape(-1)
    event = jnp.arange(events, dtype=jnp.int32)[None, :]
    listed = (flat_list[:, None] == event).astype(bf16)
    hot_match = (jnp.arange(BANDS * band, dtype=jnp.int32)[:, None] == hot_place[None, :]).astype(bf16)
    part = msg_width // 2
    msg0, msg1 = (
        jnp.dot(listed, messages[:, h * part : (h + 1) * part], preferred_element_type=f32)
        .astype(bf16)
        .reshape(n_node, slot_cap, part)
        for h in range(2)
    )
    sent = jnp.dot(listed, extra, preferred_element_type=f32)
    hot_part = jnp.dot(hot_match, messages, preferred_element_type=f32)
    hot_number = jnp.sum(hot_match.astype(f32), axis=1)
    hot_part = jnp.concatenate(
        [hot_part, jnp.broadcast_to(hot_number[:, None], (BANDS * band, 128))], axis=1
    )
    slots = jnp.arange(slot_cap, dtype=jnp.int32)
    valid = slots[None, :] < cold_count[:, None]
    row_at = (sent[:, 0] * 32.0 + sent[:, 1]).astype(jnp.int32)
    send_row = jnp.where(valid, row_at.reshape(n_node, slot_cap), -1)
    send_row = jnp.pad(send_row, ((0, 0), (0, 128 - slot_cap)), constant_values=-1)
    send_row = jnp.broadcast_to(send_row[:, None, :], (n_node, 8, 128))

    cold_total, cold_cnt, hot_sum = exchange(
        n_node, n_rep, rows_dev, msg0, msg1, send_row, hot_part.reshape(BANDS, band, msg_width + 128)
    )
    first = rep * share
    cold_number = lax.dynamic_index_in_dim(cold_cnt, rep, 0, keepdims=False)[0]
    total = jnp.concatenate([cold_total, hot_sum[:, :msg_width]], axis=0)
    count = jnp.concatenate([cold_number, hot_sum[:, msg_width]], axis=0)

    own_ids = hot_base + me * band + jnp.arange(band, dtype=jnp.int32)
    own = (own_ids[:, None] == hot_ids[None, :]).astype(f32)
    hot_state = jnp.dot(
        own, jnp.concatenate([hot_memory, cot_hot], axis=1), precision=lax.Precision.HIGHEST
    )
    mem = jnp.concatenate([lax.dynamic_slice_in_dim(memory, first, share, 0), hot_state[:, :width]], axis=0)
    cot = jnp.concatenate([lax.dynamic_slice_in_dim(cot_cold, first, share, 0), hot_state[:, width:]], axis=0)

    agg = (total / jnp.maximum(count, 1.0)[:, None]).astype(bf16)
    live = (count > 0)[:, None]
    gate_in = jnp.dot(agg, w_in, preferred_element_type=f32)
    mem_round = mem.astype(bf16)
    gate_hid = jnp.dot(mem_round, w_hid, preferred_element_type=f32)
    reset = jax.nn.sigmoid(gate_in[:, :width] + gate_hid[:, :width])
    update = jax.nn.sigmoid(gate_in[:, width : 2 * width] + gate_hid[:, width : 2 * width])
    hid_cand = gate_hid[:, 2 * width :]
    cand = jnp.tanh(gate_in[:, 2 * width :] + reset * hid_cand)
    fresh = jnp.where(live, (1.0 - update) * cand + update * mem, mem)
    cot = jnp.where(live, cot, 0.0)
    d_cand = cot * (1.0 - update) * (1.0 - cand * cand)
    d_upd = cot * (mem - cand) * update * (1.0 - update)
    d_reset = d_cand * hid_cand * reset * (1.0 - reset)
    d_input = jnp.concatenate([d_reset, d_upd, d_cand], axis=1) * GRAD_SCALE
    d_hidden = jnp.concatenate([d_reset, d_upd, d_cand * reset], axis=1) * GRAD_SCALE
    mem_wide = lax.optimization_barrier(mem_round).astype(f32)
    grad_a = jnp.dot(agg.astype(f32).T, d_input, precision=lax.Precision.HIGHEST)
    grad_b = jnp.dot(mem_wide.T, d_hidden, precision=lax.Precision.HIGHEST)
    grads = jnp.concatenate([grad_a, grad_b], axis=0)
    sizes = sizes_of(n_node, n_rep)
    ids = hot_ids - hot_base
    block, inner = lax.div(ids, band), lax.rem(ids, band)
    at_node, at_rep = lax.div(block, n_rep), lax.rem(block, n_rep)
    spot = {
        "hi": lax.div(at_node, sizes["lo"]),
        "lo": lax.rem(at_node, sizes["lo"]),
        "x": lax.div(at_rep, 2),
        "core": lax.rem(at_rep, 2),
    }
    place = sum(spot[a] * span(sizes, ORDER_HOT, i) for i, a in enumerate(ORDER_HOT)) * band + inner
    place_rows = jnp.broadcast_to(place[None, :], (8, hot_rows))
    g_rows, g_cols = grads.shape
    grads, new_cold, new_hot = finish(
        n_node, n_rep, grads.reshape(n_dev, g_rows // n_dev, g_cols), fresh[:share], fresh[share:], place_rows
    )
    grads = grads.reshape(g_rows, g_cols)
    agg_rows = w_in.shape[0]
    if band % 8:
        new_hot = jnp.take(new_hot.reshape(hot_rows, width), place, axis=0)
    return (new_cold.reshape(rows_dev, width), new_hot, grads[:agg_rows], grads[agg_rows:])


def solution(mesh):
    both = P(("node", "rep"))
    in_specs = (
        P("node", None),
        P(),
        P("node", None),
        P(),
        both,
        both,
        both,
        P(("node", "rep"), None),
        P(("node", "rep"), None),
        both,
        P(),
        P(),
        P(),
        P(),
        P(),
        P(),
        P(),
    )
    out_specs = (P("node", None), P(), P(), P())
    return jax.shard_map(on_device, mesh=mesh, in_specs=in_specs, out_specs=out_specs, check_vma=False)
```

```python
import functools
import math

import jax
import jax.numpy as jnp
from jax import lax
from jax.experimental import pallas as pl
from jax.experimental.pallas import tpu as pltpu
from jax.sharding import PartitionSpec as P

GRAD_SCALE = 1.0 / 64.0
BANDS = 4
MESH = pl.DeviceIdType.MESH
VMEM = pl.BlockSpec(memory_space=pltpu.VMEM)


def greet(devices):
    barrier = pltpu.get_barrier_semaphore()
    for device in devices:
        pl.semaphore_signal(barrier, inc=1, device_id=device, device_id_type=MESH)
    pl.semaphore_wait(barrier, len(devices))


def push(src, dst, send_sem, recv_sem, device):
    copy = pltpu.make_async_remote_copy(
        src_ref=src, dst_ref=dst, send_sem=send_sem, recv_sem=recv_sem, device_id=device, device_id_type=MESH
    )
    copy.start()
    return copy


def exchange_kernel(
    n_node, n_rep,
    messages_ref, list_ref, number_ref, dst_ref, ids_ref, memory_any, cot_any, hot_memory_any, hot_cot_any,
    sum_out, cnt_out, hot_out, mem_out, cot_out,
    msg0_ref, msg1_ref, rows_ref, hot_ref, hot_state, own_sem,
    recv0, recv1, rows_recv, hot_recv, sums, cnts, core_recv, x_send, x_recv, cnt_core, cnt_send, cnt_x,
    msg_s, msg_r, row_s, row_r, hot_s, hot_r, core_s, core_r, x_s, x_r, cc_s, cc_r, cx_s, cx_r,
):
    nx = n_rep // 2
    n_dev = n_node * n_rep
    node = lax.axis_index("node")
    rep = lax.axis_index("rep")
    core = lax.rem(rep, 2)
    xi = lax.div(rep, 2)
    me = node * n_rep + rep
    cap, part = msg0_ref.shape[1:]
    share = sum_out.shape[0]
    rows_dev = share * n_rep
    events = messages_ref.shape[0]
    hot_rows = ids_ref.shape[1]
    band = hot_rows // n_dev
    hot_base = n_node * rows_dev
    f32, bf16 = jnp.float32, jnp.bfloat16
    nlo = n_node // 4
    hi, lo = lax.div(node, nlo), lax.rem(node, nlo)
    steps = [(a, b) for a in (2, 1, 3, 0) for b in range(nlo) if a or b]

    def node_at(a, b):
        return lax.rem(hi + a, 4) * nlo + lax.rem(lo + b, nlo)

    first = pl.multiple_of(rep * share, share)
    own_copies = [
        pltpu.make_async_copy(src, dst, own_sem.at[i])
        for i, (src, dst) in enumerate(
            (
                (memory_any.at[pl.ds(first, share)], mem_out.at[pl.ds(0, share)]),
                (cot_any.at[pl.ds(first, share)], cot_out.at[pl.ds(0, share)]),
                (hot_memory_any, hot_state.at[0]),
                (hot_cot_any, hot_state.at[1]),
            )
        )
    ]
    for copy in own_copies:
        copy.start()

    def at_linear(k):
        other = lax.rem(me + k, n_dev)
        return (lax.div(other, n_rep), lax.rem(other, n_rep))

    other_core = (node, xi * 2 + 1 - core)

    def at_x(k):
        return (node, lax.rem(xi + k, nx) * 2 + core)

    greet(
        [(node_at(a, b), rep) for a, b in steps]
        + [other_core]
        + [at_x(k) for k in range(1, nx)]
        + [at_linear(j) for j in range(1, BANDS)]
        + [at_linear(n_dev - j) for j in range(1, BANDS)]
    )

    dst = dst_ref[...]
    local_row = lax.rem(dst, rows_dev)
    which = lax.broadcasted_iota(jnp.int32, (8, events), 0)
    high = lax.div(local_row, 32)
    digits = jnp.where(which == 0, high, jnp.where(which == 1, local_row - high * 32, 0))
    digits = digits.astype(f32).astype(bf16)
    slot = lax.broadcasted_iota(jnp.int32, (1, cap), 1)

    def build(other):
        listed = lax.broadcasted_iota(jnp.int32, (events, cap), 0) == list_ref[pl.ds(other, 1), :]
        listed = jnp.where(listed, 1.0, 0.0).astype(bf16)
        block = lax.dot_general(
            listed, messages_ref[...], (((0,), (0,)), ((), ())), preferred_element_type=f32
        ).astype(bf16)
        msg0_ref[other] = block[:, :part]
        msg1_ref[other] = block[:, part:]
        found = jnp.dot(digits, listed, preferred_element_type=f32)
        row = (found[0:1] * 32.0 + found[1:2]).astype(jnp.int32)
        row = jnp.where(slot < number_ref[pl.ds(other, 1), :], row, -1)
        rows_ref[other, :, :cap] = jnp.broadcast_to(row, (8, cap))

    arrivals = {}
    for k, (a, b) in enumerate(steps):
        other = node_at(a, b)
        build(other)
        arrivals["row", k] = push(rows_ref.at[other], rows_recv.at[node], row_s.at[k], row_r.at[k], (other, rep))
        arrivals[0, k] = push(msg0_ref.at[other], recv0.at[node], msg_s.at[0, k], msg_r.at[0, k], (other, rep))
    for k, (a, b) in enumerate(steps):
        other = node_at(a, b)
        arrivals[1, k] = push(msg1_ref.at[other], recv1.at[node], msg_s.at[1, k], msg_r.at[1, k], (other, rep))
    sent = list(arrivals.values())

    place = dst - hot_base - me * band
    place = jnp.where(place < 0, place + hot_rows, place)
    place = jnp.where(dst >= hot_base, place, -1)
    match = jnp.where(lax.broadcasted_iota(jnp.int32, (BANDS * band, events), 0) == place, 1.0, 0.0)
    hot_part = jnp.dot(match.astype(bf16), messages_ref[...], preferred_element_type=f32)
    hot_number = jnp.sum(match, axis=1, keepdims=True)
    for j in range(BANDS):
        hot_ref[j, :, : 2 * part] = hot_part[j * band : (j + 1) * band]
        hot_ref[j, :, 2 * part :] = jnp.broadcast_to(hot_number[j * band : (j + 1) * band], (band, 128))
    hots = [
        push(hot_ref.at[j], hot_recv.at[j - 1], hot_s.at[j - 1], hot_r.at[j - 1], at_linear(j))
        for j in range(1, BANDS)
    ]
    sent += hots
    build(node)
    for copy in own_copies:
        copy.wait()
    own_rows = max(band, 8)
    own = lax.broadcasted_iota(jnp.int32, (own_rows, hot_rows), 0) + (hot_base + me * band) == ids_ref[...]
    own = jnp.where(own, 1.0, 0.0)
    for i, out in enumerate((mem_out, cot_out)):
        rows = jnp.dot(own, hot_state[i], precision=lax.Precision.HIGHEST, preferred_element_type=f32)
        out[share : share + band] = rows[:band]

    sums[...] = jnp.zeros_like(sums)
    cnts[...] = jnp.zeros_like(cnts)
    ones = jnp.ones((8, cap), jnp.bfloat16)

    def add_block(h, rows, block):
        for s in range(n_rep):
            spot = lax.broadcasted_iota(jnp.int32, (share, cap), 0) + s * share
            equal = jnp.where(spot == rows, 1.0, 0.0).astype(jnp.bfloat16)
            sums[h, s // 2, s % 2] += jnp.dot(equal, block, preferred_element_type=jnp.float32)
            if h == 0:
                cnts[s] += lax.dot_general(
                    ones, equal, (((1,), (1,)), ((), ())), preferred_element_type=jnp.float32
                )

    crossing = [[], []]
    counts = []
    for h, (mine, got) in enumerate(((msg0_ref, recv0), (msg1_ref, recv1))):
        add_block(h, rows_ref[node, 0:1, :cap], mine[node])
        for k, (a, b) in enumerate(steps):
            if h == 0:
                arrivals["row", k].wait_recv()
            arrivals[h, k].wait_recv()
            origin = node_at(4 - a, nlo - b)
            add_block(h, rows_recv[origin, 0:1, :cap], got[origin])
        halves = []
        for k in [*range(1, nx), 0]:
            p = lax.rem(xi + k, nx)
            copy = push(sums.at[h, p, 1 - core], core_recv.at[h, k], core_s.at[h, k], core_r.at[h, k], other_core)
            halves.append((k, p, copy))
        if h == 0:
            cnt_copy = push(cnts, cnt_core, cc_s, cc_r, other_core)
            sent.append(cnt_copy)
        for k, p, copy in halves:
            copy.wait_recv()
            sent.append(copy)
            if k:
                x_send[h, k - 1] = sums[h, p, core] + core_recv[h, k]
                crossing[h].append(
                    push(x_send.at[h, k - 1], x_recv.at[h, k - 1], x_s.at[h, k - 1], x_r.at[h, k - 1], at_x(k))
                )
        if h == 0:
            cnt_copy.wait_recv()
            cnt_send[...] = cnts[...] + cnt_core[...]
            counts = [
                push(cnt_send, cnt_x.at[k - 1], cx_s.at[k - 1], cx_r.at[k - 1], at_x(k)) for k in range(1, nx)
            ]
    for copy in hots:
        copy.wait_recv()
    hot_out[...] = hot_ref[0] + hot_recv[0] + hot_recv[1] + hot_recv[2]
    number = cnt_send[...]
    for k, copy in enumerate(counts):
        copy.wait_recv()
        number += cnt_x[k]
    cnt_out[...] = number
    for h in range(2):
        total = sums[h, xi, core] + core_recv[h, 0]
        for k, copy in enumerate(crossing[h]):
            copy.wait_recv()
            total += x_recv[h, k]
        sum_out[:, h * part : (h + 1) * part] = total
    for copy in [*sent, *crossing[0], *crossing[1], *counts]:
        copy.wait_send()


def exchange(n_node, n_rep, messages, lists, numbers, dst, ids, memory, cot, hot_memory, hot_cot):
    nx = n_rep // 2
    cap = lists.shape[1]
    part = messages.shape[1] // 2
    rows_dev, width = memory.shape
    hot_rows = hot_memory.shape[0]
    band = hot_rows // (n_node * n_rep)
    hot_width = 2 * part + 128
    share = rows_dev // n_rep
    dma = pltpu.SemaphoreType.DMA
    f32 = jnp.float32
    block = pltpu.VMEM((n_node, cap, part), messages.dtype)
    row_block = pltpu.VMEM((n_node, 8, 128), jnp.int32)
    return pl.pallas_call(
        functools.partial(exchange_kernel, n_node, n_rep),
        out_shape=(
            jax.ShapeDtypeStruct((share, 2 * part), f32),
            jax.ShapeDtypeStruct((n_rep, 8, share), f32),
            jax.ShapeDtypeStruct((band, hot_width), f32),
            jax.ShapeDtypeStruct((share + band, width), f32),
            jax.ShapeDtypeStruct((share + band, width), f32),
        ),
        in_specs=[VMEM] * 5 + [pl.BlockSpec(memory_space=pl.ANY)] * 4,
        out_specs=(VMEM,) * 5,
        scratch_shapes=[
            block,
            block,
            row_block,
            pltpu.VMEM((BANDS, band, hot_width), f32),
            pltpu.VMEM((2, hot_rows, width), f32),
            dma((4,)),
            block,
            block,
            row_block,
            pltpu.VMEM((BANDS - 1, band, hot_width), f32),
            pltpu.VMEM((2, nx, 2, share, part), f32),
            pltpu.VMEM((n_rep, 8, share), f32),
            pltpu.VMEM((2, nx, share, part), f32),
            pltpu.VMEM((2, nx - 1, share, part), f32),
            pltpu.VMEM((2, nx - 1, share, part), f32),
            pltpu.VMEM((n_rep, 8, share), f32),
            pltpu.VMEM((n_rep, 8, share), f32),
            pltpu.VMEM((nx - 1, n_rep, 8, share), f32),
            dma((2, n_node)), dma((2, n_node)), dma((n_node,)), dma((n_node,)),
            dma((BANDS - 1,)), dma((BANDS - 1,)),
            dma((2, nx)), dma((2, nx)),
            dma((2, nx - 1)), dma((2, nx - 1)),
            dma, dma,
            dma((nx - 1,)), dma((nx - 1,)),
        ],
        compiler_params=pltpu.CompilerParams(
            collective_id=0, has_side_effects=True, vmem_limit_bytes=40 * 1024 * 1024
        ),
    )(messages, lists, numbers, dst, ids, memory, cot, hot_memory, hot_cot)


ORDER_A = ("core", "x", "lo", "hi")
ORDER_B = ("core", "lo", "x", "hi")
ORDER_HOT = ("core", "lo", "hi", "x")
LANES = 128


def sizes_of(n_node, n_rep):
    return {"core": 2, "x": n_rep // 2, "lo": n_node // 4, "hi": 4}


def span(sizes, order, phase):
    return math.prod(sizes[a] for a in order[phase + 1 :])


def parts_of(columns):
    return [(first, ORDER_B if i % 2 else ORDER_A) for i, first in enumerate(range(0, columns, LANES))]


def finish_kernel(n_node, n_rep, hot_base, g_ref, cold_ref, hot_ref, ids_ref, og, ocold, new_hot, *scratch):
    sizes = sizes_of(n_node, n_rep)
    parts = parts_of(g_ref.shape[2])
    send_sem, recv_sem = scratch[:2]
    buffers = scratch[2 : 2 + 8 * len(parts)]
    band, width = hot_ref.shape
    tidy = band % 8 == 0
    ohot, pieces = scratch[2 + 8 * len(parts) :] if tidy else (new_hot, None)
    node = lax.axis_index("node")
    rep = lax.axis_index("rep")
    nlo = sizes["lo"]
    mine = {"core": lax.rem(rep, 2), "x": lax.div(rep, 2), "lo": lax.rem(node, nlo), "hi": lax.div(node, nlo)}

    def peer(axis, k):
        spot = dict(mine)
        spot[axis] = lax.rem(mine[axis] + k, sizes[axis])
        return (spot["hi"] * nlo + spot["lo"], spot["x"] * 2 + spot["core"])

    greet([peer(axis, k) for axis in ORDER_A for k in range(1, sizes[axis])])

    everything = []

    def ship(src, dst, device):
        i = len(everything)
        copy = push(src, dst, send_sem.at[i], recv_sem.at[i], device)
        everything.append(copy)
        return copy

    def arrive(copies):
        for copy in copies:
            copy.wait_recv()

    def held(part, phase):
        first, order = parts[part]
        if phase == 0:
            return lambda i, n: g_ref.at[pl.ds(i, n), :, pl.ds(first, LANES)]
        acc = buffers[8 * part + 2 * (phase - 1) + 1]
        return lambda i, n: acc.at[pl.ds(i, n)]

    def scatter_start(part, phase):
        order = parts[part][1]
        axis = order[phase]
        size, n = sizes[axis], span(sizes, order, phase)
        view, recv = held(part, phase), buffers[8 * part + 2 * phase]
        return [
            ship(view(lax.rem(mine[axis] + k, size) * n, n), recv.at[k - 1], peer(axis, k)) for k in range(1, size)
        ]

    def scatter_end(part, phase, copies):
        order = parts[part][1]
        axis = order[phase]
        n = span(sizes, order, phase)
        recv, acc = buffers[8 * part + 2 * phase], buffers[8 * part + 2 * phase + 1]
        total = held(part, phase)(mine[axis] * n, n)[...]
        for k, copy in enumerate(copies):
            copy.wait_recv()
            total = total + recv[k]
        acc[...] = total

    def prefix(order, phase):
        return sum(mine[order[i]] * span(sizes, order, i) for i in range(phase + 1))

    def gather_start(part, phase):
        first, order = parts[part]
        axis = order[phase]
        where = og.at[pl.ds(prefix(order, phase), span(sizes, order, phase)), :, pl.ds(first, LANES)]
        return [ship(where, where, peer(axis, k)) for k in range(1, sizes[axis])]

    def hot_start(phase):
        axis = ORDER_HOT[phase]
        spot = [mine[a] if a in ORDER_HOT[: phase + 1] else slice(None) for a in ("hi", "lo", "x", "core")]
        where = ohot.at[tuple(spot)]
        return [ship(where, where, peer(axis, k)) for k in range(1, sizes[axis])]

    everyone = range(len(parts))
    flying = [scatter_start(part, 0) for part in everyone]
    ocold[mine["x"], mine["core"]] = cold_ref[...]
    ohot[mine["hi"], mine["lo"], mine["x"], mine["core"]] = hot_ref[...]
    cold_place = ocold.at[mine["x"], mine["core"]]
    hot_copies = hot_start(3)
    cold_copies = [ship(cold_place, cold_place, peer("x", k)) for k in range(1, sizes["x"])]

    for phase in range(4):
        for part in everyone:
            scatter_end(part, phase, flying[part])
            if phase < 3:
                flying[part] = scatter_start(part, phase + 1)
            else:
                first, order = parts[part]
                og[pl.ds(prefix(order, 3), 1), :, first : first + LANES] = buffers[8 * part + 7][...]
                flying[part] = gather_start(part, 3)
        arrive(hot_copies)
        hot_copies = hot_start(2 - phase) if phase < 3 else []
        if phase == 1:
            arrive(cold_copies)
            side = ocold.at[:, mine["core"]]
            cold_copies = [ship(side, side, peer("core", 1))]
    if tidy:
        hot_rows = new_hot.shape[0]
        rows = ohot[...].reshape(hot_rows, width)
        top = rows.astype(jnp.bfloat16)
        rest = rows - top.astype(jnp.float32)
        middle = rest.astype(jnp.bfloat16)
        pieces[:, :width] = top
        pieces[:, width : 2 * width] = middle
        pieces[:, 2 * width :] = (rest - middle.astype(jnp.float32)).astype(jnp.bfloat16)

    def permute_hot(part):
        step = new_hot.shape[0] // 4
        chosen = lax.broadcasted_iota(jnp.int32, (new_hot.shape[0], step), 0)
        chosen = chosen == ids_ref[:, part * step : (part + 1) * step] - hot_base
        got = lax.dot_general(
            jnp.where(chosen, 1.0, 0.0).astype(jnp.bfloat16),
            pieces[...],
            (((0,), (0,)), ((), ())),
            preferred_element_type=jnp.float32,
        )
        new_hot[part * step : (part + 1) * step] = got[:, :width] + got[:, width : 2 * width] + got[:, 2 * width :]

    for phase in (3, 2, 1, 0):
        for part in everyone:
            arrive(flying[part])
            flying[part] = gather_start(part, phase - 1) if phase else []
        if tidy:
            permute_hot(3 - phase)
    arrive(cold_copies)
    for copy in everything:
        copy.wait_send()


def finish(n_node, n_rep, hot_base, grads, cold, hot, ids):
    sizes = sizes_of(n_node, n_rep)
    f32 = jnp.float32
    n_dev, piece, columns = grads.shape
    parts = parts_of(columns)
    steps = sum(s - 1 for s in sizes.values())
    n_sems = 2 * steps * len(parts) + steps + sizes["x"] - 1 + 1
    scratch = [pltpu.SemaphoreType.DMA((n_sems,)), pltpu.SemaphoreType.DMA((n_sems,))]
    for first, order in parts:
        for phase in range(4):
            block = (span(sizes, order, phase), piece, LANES)
            scratch += [pltpu.VMEM((sizes[order[phase]] - 1, *block), f32), pltpu.VMEM(block, f32)]
    band, width = hot.shape
    hot_rows = ids.shape[1]
    blocks = (sizes["hi"], sizes["lo"], sizes["x"], 2, band, width)
    out_hot = jax.ShapeDtypeStruct(blocks, f32)
    if band % 8 == 0:
        out_hot = jax.ShapeDtypeStruct((hot_rows, width), f32)
        scratch += [pltpu.VMEM(blocks, f32), pltpu.VMEM((hot_rows, 3 * width), jnp.bfloat16)]
    return pl.pallas_call(
        functools.partial(finish_kernel, n_node, n_rep, hot_base),
        out_shape=(
            jax.ShapeDtypeStruct(grads.shape, f32),
            jax.ShapeDtypeStruct((sizes["x"], 2, *cold.shape), f32),
            out_hot,
        ),
        in_specs=[VMEM] * 4,
        out_specs=(VMEM,) * 3,
        scratch_shapes=scratch,
        compiler_params=pltpu.CompilerParams(
            collective_id=1, has_side_effects=True, vmem_limit_bytes=40 * 1024 * 1024
        ),
    )(grads, cold, hot, ids)


def on_device(
    memory,
    hot_memory,
    cot_cold,
    cot_hot,
    src_local,
    dst_ids,
    times,
    edge_feat,
    cold_list,
    cold_count,
    hot_ids,
    time_freq,
    time_phase,
    w_msg,
    b_msg,
    w_in,
    w_hid,
):
    f32, bf16 = jnp.float32, jnp.bfloat16
    n_node = lax.axis_size("node")
    n_rep = lax.axis_size("rep")
    n_dev = n_node * n_rep
    rows_dev, width = memory.shape
    hot_rows = hot_memory.shape[0]
    events = src_local.shape[0]
    msg_width = w_msg.shape[1]
    band = hot_rows // n_dev
    share = rows_dev // n_rep
    rep = lax.axis_index("rep")
    hot_base = n_node * rows_dev

    pick = (src_local[:, None] == jnp.arange(rows_dev, dtype=jnp.int32)[None, :]).astype(bf16)
    src_mem = jnp.dot(pick, memory.astype(bf16), preferred_element_type=f32).astype(bf16)
    enc = jnp.cos(times.astype(f32)[:, None] * time_freq[None, :] + time_phase[None, :]).astype(bf16)
    raw = jnp.concatenate([src_mem, edge_feat, enc], axis=1)
    messages = jax.nn.silu(jnp.dot(raw, w_msg, preferred_element_type=f32) + b_msg[None, :]).astype(bf16)

    ids_row = hot_ids.reshape(1, hot_rows)
    cold_total, cold_cnt, hot_sum, mem, cot = exchange(
        n_node,
        n_rep,
        messages,
        cold_list,
        cold_count.reshape(n_node, 1),
        dst_ids.reshape(1, events),
        ids_row,
        memory,
        cot_cold,
        hot_memory,
        cot_hot,
    )
    cold_number = lax.dynamic_index_in_dim(cold_cnt, rep, 0, keepdims=False)[0]
    total = jnp.concatenate([cold_total, hot_sum[:, :msg_width]], axis=0)
    count = jnp.concatenate([cold_number, hot_sum[:, msg_width]], axis=0)

    agg = (total / jnp.maximum(count, 1.0)[:, None]).astype(bf16)
    live = (count > 0)[:, None]
    gate_in = jnp.dot(agg, w_in, preferred_element_type=f32)
    mem_round = mem.astype(bf16)
    gate_hid = jnp.dot(mem_round, w_hid, preferred_element_type=f32)
    reset = jax.nn.sigmoid(gate_in[:, :width] + gate_hid[:, :width])
    update = jax.nn.sigmoid(gate_in[:, width : 2 * width] + gate_hid[:, width : 2 * width])
    hid_cand = gate_hid[:, 2 * width :]
    cand = jnp.tanh(gate_in[:, 2 * width :] + reset * hid_cand)
    fresh = jnp.where(live, (1.0 - update) * cand + update * mem, mem)
    cot = jnp.where(live, cot, 0.0)
    d_cand = cot * (1.0 - update) * (1.0 - cand * cand)
    d_upd = cot * (mem - cand) * update * (1.0 - update)
    d_reset = d_cand * hid_cand * reset * (1.0 - reset)
    d_input = jnp.concatenate([d_reset, d_upd, d_cand], axis=1) * GRAD_SCALE
    d_hidden = jnp.concatenate([d_reset, d_upd, d_cand * reset], axis=1) * GRAD_SCALE
    mem_wide = lax.optimization_barrier(mem_round).astype(f32)
    grad_a = jnp.dot(agg.astype(f32).T, d_input, precision=lax.Precision.HIGHEST)
    grad_b = jnp.dot(mem_wide.T, d_hidden, precision=lax.Precision.HIGHEST)
    grads = jnp.concatenate([grad_a, grad_b], axis=0)
    g_rows, g_cols = grads.shape
    grads, new_cold, new_hot = finish(
        n_node, n_rep, hot_base, grads.reshape(n_dev, g_rows // n_dev, g_cols), fresh[:share], fresh[share:], ids_row
    )
    grads = grads.reshape(g_rows, g_cols)
    agg_rows = w_in.shape[0]
    if band % 8:
        new_hot = jnp.take(new_hot.reshape(hot_rows, width), hot_ids - hot_base, axis=0)
    return (new_cold.reshape(rows_dev, width), new_hot, grads[:agg_rows], grads[agg_rows:])


def solution(mesh):
    both = P(("node", "rep"))
    in_specs = (
        P("node", None),
        P(),
        P("node", None),
        P(),
        both,
        both,
        both,
        P(("node", "rep"), None),
        P(("node", "rep"), None),
        both,
        P(),
        P(),
        P(),
        P(),
        P(),
        P(),
        P(),
    )
    out_specs = (P("node", None), P(), P(), P())
    return jax.shard_map(on_device, mesh=mesh, in_specs=in_specs, out_specs=out_specs, check_vma=False)
```

```python
import functools
import math

import jax
import jax.numpy as jnp
from jax import lax
from jax.experimental import pallas as pl
from jax.experimental.pallas import tpu as pltpu
from jax.sharding import PartitionSpec as P

GRAD_SCALE = 1.0 / 64.0
BANDS = 4
MESH = pl.DeviceIdType.MESH
VMEM = pl.BlockSpec(memory_space=pltpu.VMEM)


def greet(devices):
    barrier = pltpu.get_barrier_semaphore()
    for device in devices:
        pl.semaphore_signal(barrier, inc=1, device_id=device, device_id_type=MESH)
    pl.semaphore_wait(barrier, len(devices))


def push(src, dst, send_sem, recv_sem, device):
    copy = pltpu.make_async_remote_copy(
        src_ref=src, dst_ref=dst, send_sem=send_sem, recv_sem=recv_sem, device_id=device, device_id_type=MESH
    )
    copy.start()
    return copy


def exchange_kernel(
    n_node, n_rep,
    messages_ref, list_ref, number_ref, dst_ref, ids_ref, memory_any, cot_any, hot_memory_any, hot_cot_any,
    sum_out, cnt_out, hot_out, mem_out, cot_out,
    rows_ref, hot_ref, hot_state, own_sem,
    rows_recv, hot_recv, cnts, cnt_core, cnt_send, cnt_x,
    msg_s, msg_r, row_s, row_r, hot_s, hot_r, core_s, core_r, x_s, x_r, cc_s, cc_r, cx_s, cx_r,
    *chunked,
):
    nx = n_rep // 2
    n_dev = n_node * n_rep
    node = lax.axis_index("node")
    rep = lax.axis_index("rep")
    core = lax.rem(rep, 2)
    xi = lax.div(rep, 2)
    me = node * n_rep + rep
    cap = list_ref.shape[1]
    msg_width = messages_ref.shape[1]
    cuts = cuts_of(msg_width)
    msg_refs, recvs, sums, core_recv, x_send, x_recv = (
        chunked[i * len(cuts) : (i + 1) * len(cuts)] for i in range(6)
    )
    share = sum_out.shape[0]
    rows_dev = share * n_rep
    events = messages_ref.shape[0]
    hot_rows = ids_ref.shape[1]
    band = hot_rows // n_dev
    hot_base = n_node * rows_dev
    f32, bf16 = jnp.float32, jnp.bfloat16
    nlo = n_node // 4
    hi, lo = lax.div(node, nlo), lax.rem(node, nlo)
    steps = [(a, b) for a in (2, 1, 3, 0) for b in range(nlo) if a or b]

    def node_at(a, b):
        return lax.rem(hi + a, 4) * nlo + lax.rem(lo + b, nlo)

    first = pl.multiple_of(rep * share, share)
    own_copies = [
        pltpu.make_async_copy(src, dst, own_sem.at[i])
        for i, (src, dst) in enumerate(
            (
                (memory_any.at[pl.ds(first, share)], mem_out.at[pl.ds(0, share)]),
                (cot_any.at[pl.ds(first, share)], cot_out.at[pl.ds(0, share)]),
                (hot_memory_any, hot_state.at[0]),
                (hot_cot_any, hot_state.at[1]),
            )
        )
    ]
    for copy in own_copies:
        copy.start()

    def at_linear(k):
        other = lax.rem(me + k, n_dev)
        return (lax.div(other, n_rep), lax.rem(other, n_rep))

    other_core = (node, xi * 2 + 1 - core)

    def at_x(k):
        return (node, lax.rem(xi + k, nx) * 2 + core)

    greet(
        [(node_at(a, b), rep) for a, b in steps]
        + [other_core]
        + [at_x(k) for k in range(1, nx)]
        + [at_linear(j) for j in range(1, BANDS)]
        + [at_linear(n_dev - j) for j in range(1, BANDS)]
    )

    dst = dst_ref[...]
    local_row = lax.rem(dst, rows_dev)
    which = lax.broadcasted_iota(jnp.int32, (8, events), 0)
    high = lax.div(local_row, 32)
    digits = jnp.where(which == 0, high, jnp.where(which == 1, local_row - high * 32, 0))
    digits = digits.astype(f32).astype(bf16)
    slot = lax.broadcasted_iota(jnp.int32, (1, cap), 1)

    def build(other):
        listed = lax.broadcasted_iota(jnp.int32, (events, cap), 0) == list_ref[pl.ds(other, 1), :]
        listed = jnp.where(listed, 1.0, 0.0).astype(bf16)
        block = lax.dot_general(
            listed, messages_ref[...], (((0,), (0,)), ((), ())), preferred_element_type=f32
        ).astype(bf16)
        for ref, (begin, size) in zip(msg_refs, cuts):
            ref[other] = block[:, begin : begin + size]
        found = jnp.dot(digits, listed, preferred_element_type=f32)
        row = (found[0:1] * 32.0 + found[1:2]).astype(jnp.int32)
        row = jnp.where(slot < number_ref[pl.ds(other, 1), :], row, -1)
        rows_ref[other, :, :cap] = jnp.broadcast_to(row, (8, cap))

    arrivals = {}
    for k, (a, b) in enumerate(steps):
        other = node_at(a, b)
        build(other)
        arrivals["row", k] = push(rows_ref.at[other], rows_recv.at[node], row_s.at[k], row_r.at[k], (other, rep))
        arrivals[0, k] = push(
            msg_refs[0].at[other], recvs[0].at[node], msg_s.at[0, k], msg_r.at[0, k], (other, rep)
        )
    for h in range(1, len(cuts)):
        for k, (a, b) in enumerate(steps):
            other = node_at(a, b)
            arrivals[h, k] = push(
                msg_refs[h].at[other], recvs[h].at[node], msg_s.at[h, k], msg_r.at[h, k], (other, rep)
            )
    sent = list(arrivals.values())

    place = dst - hot_base - me * band
    place = jnp.where(place < 0, place + hot_rows, place)
    place = jnp.where(dst >= hot_base, place, -1)
    match = jnp.where(lax.broadcasted_iota(jnp.int32, (BANDS * band, events), 0) == place, 1.0, 0.0)
    hot_part = jnp.dot(match.astype(bf16), messages_ref[...], preferred_element_type=f32)
    hot_number = jnp.sum(match, axis=1, keepdims=True)
    for j in range(BANDS):
        hot_ref[j, :, :msg_width] = hot_part[j * band : (j + 1) * band]
        hot_ref[j, :, msg_width:] = jnp.broadcast_to(hot_number[j * band : (j + 1) * band], (band, 128))
    hots = [
        push(hot_ref.at[j], hot_recv.at[j - 1], hot_s.at[j - 1], hot_r.at[j - 1], at_linear(j))
        for j in range(1, BANDS)
    ]
    sent += hots
    build(node)
    for copy in own_copies:
        copy.wait()
    own_rows = max(band, 8)
    own = lax.broadcasted_iota(jnp.int32, (own_rows, hot_rows), 0) + (hot_base + me * band) == ids_ref[...]
    own = jnp.where(own, 1.0, 0.0)
    for i, out in enumerate((mem_out, cot_out)):
        rows = jnp.dot(own, hot_state[i], precision=lax.Precision.HIGHEST, preferred_element_type=f32)
        out[share : share + band] = rows[:band]

    for ref in sums:
        ref[...] = jnp.zeros_like(ref)
    cnts[...] = jnp.zeros_like(cnts)
    ones = jnp.ones((8, cap), jnp.bfloat16)

    def add_block(h, rows, block):
        for s in range(n_rep):
            spot = lax.broadcasted_iota(jnp.int32, (share, cap), 0) + s * share
            equal = jnp.where(spot == rows, 1.0, 0.0).astype(jnp.bfloat16)
            sums[h][s // 2, s % 2] += jnp.dot(equal, block, preferred_element_type=jnp.float32)
            if h == 0:
                cnts[s] += lax.dot_general(
                    ones, equal, (((1,), (1,)), ((), ())), preferred_element_type=jnp.float32
                )

    crossing = [[] for _ in cuts]
    counts = []
    for h, (mine, got) in enumerate(zip(msg_refs, recvs)):
        add_block(h, rows_ref[node, 0:1, :cap], mine[node])
        for k, (a, b) in enumerate(steps):
            if h == 0:
                arrivals["row", k].wait_recv()
            arrivals[h, k].wait_recv()
            origin = node_at(4 - a, nlo - b)
            add_block(h, rows_recv[origin, 0:1, :cap], got[origin])
        halves = []
        for k in [*range(1, nx), 0]:
            p = lax.rem(xi + k, nx)
            copy = push(sums[h].at[p, 1 - core], core_recv[h].at[k], core_s.at[h, k], core_r.at[h, k], other_core)
            halves.append((k, p, copy))
        if h == 0:
            cnt_copy = push(cnts, cnt_core, cc_s, cc_r, other_core)
            sent.append(cnt_copy)
        for k, p, copy in halves:
            copy.wait_recv()
            sent.append(copy)
            if k:
                x_send[h][k - 1] = sums[h][p, core] + core_recv[h][k]
                crossing[h].append(
                    push(x_send[h].at[k - 1], x_recv[h].at[k - 1], x_s.at[h, k - 1], x_r.at[h, k - 1], at_x(k))
                )
        if h == 0:
            cnt_copy.wait_recv()
            cnt_send[...] = cnts[...] + cnt_core[...]
            counts = [
                push(cnt_send, cnt_x.at[k - 1], cx_s.at[k - 1], cx_r.at[k - 1], at_x(k)) for k in range(1, nx)
            ]
    for copy in hots:
        copy.wait_recv()
    hot_out[...] = hot_ref[0] + hot_recv[0] + hot_recv[1] + hot_recv[2]
    number = cnt_send[...]
    for k, copy in enumerate(counts):
        copy.wait_recv()
        number += cnt_x[k]
    cnt_out[...] = number
    for h, (begin, size) in enumerate(cuts):
        total = sums[h][xi, core] + core_recv[h][0]
        for k, copy in enumerate(crossing[h]):
            copy.wait_recv()
            total += x_recv[h][k]
        sum_out[:, begin : begin + size] = total
    for copy in [*sent, *sum(crossing, []), *counts]:
        copy.wait_send()


def cuts_of(width):
    return [(0, width // 2), (width // 2, width // 4), (3 * width // 4, width // 4)]


def exchange(n_node, n_rep, messages, lists, numbers, dst, ids, memory, cot, hot_memory, hot_cot):
    nx = n_rep // 2
    cap = lists.shape[1]
    msg_width = messages.shape[1]
    cuts = cuts_of(msg_width)
    rows_dev, width = memory.shape
    hot_rows = hot_memory.shape[0]
    band = hot_rows // (n_node * n_rep)
    hot_width = msg_width + 128
    share = rows_dev // n_rep
    dma = pltpu.SemaphoreType.DMA
    f32 = jnp.float32

    def chunked(*shape, dtype=jnp.float32):
        return [pltpu.VMEM((*shape, size), dtype) for _, size in cuts]

    row_block = pltpu.VMEM((n_node, 8, 128), jnp.int32)
    return pl.pallas_call(
        functools.partial(exchange_kernel, n_node, n_rep),
        out_shape=(
            jax.ShapeDtypeStruct((share, msg_width), f32),
            jax.ShapeDtypeStruct((n_rep, 8, share), f32),
            jax.ShapeDtypeStruct((band, hot_width), f32),
            jax.ShapeDtypeStruct((share + band, width), f32),
            jax.ShapeDtypeStruct((share + band, width), f32),
        ),
        in_specs=[VMEM] * 5 + [pl.BlockSpec(memory_space=pl.ANY)] * 4,
        out_specs=(VMEM,) * 5,
        scratch_shapes=[
            row_block,
            pltpu.VMEM((BANDS, band, hot_width), f32),
            pltpu.VMEM((2, hot_rows, width), f32),
            dma((4,)),
            row_block,
            pltpu.VMEM((BANDS - 1, band, hot_width), f32),
            pltpu.VMEM((n_rep, 8, share), f32),
            pltpu.VMEM((n_rep, 8, share), f32),
            pltpu.VMEM((n_rep, 8, share), f32),
            pltpu.VMEM((nx - 1, n_rep, 8, share), f32),
            dma((len(cuts), n_node)), dma((len(cuts), n_node)), dma((n_node,)), dma((n_node,)),
            dma((BANDS - 1,)), dma((BANDS - 1,)),
            dma((len(cuts), nx)), dma((len(cuts), nx)),
            dma((len(cuts), nx - 1)), dma((len(cuts), nx - 1)),
            dma, dma,
            dma((nx - 1,)), dma((nx - 1,)),
            *chunked(n_node, cap, dtype=messages.dtype),
            *chunked(n_node, cap, dtype=messages.dtype),
            *chunked(nx, 2, share),
            *chunked(nx, share),
            *chunked(nx - 1, share),
            *chunked(nx - 1, share),
        ],
        compiler_params=pltpu.CompilerParams(
            collective_id=0, has_side_effects=True, vmem_limit_bytes=40 * 1024 * 1024
        ),
    )(messages, lists, numbers, dst, ids, memory, cot, hot_memory, hot_cot)


ORDER_A = ("core", "x", "lo", "hi")
ORDER_B = ("core", "lo", "x", "hi")
ORDER_HOT = ("core", "lo", "hi", "x")
LANES = 128


def sizes_of(n_node, n_rep):
    return {"core": 2, "x": n_rep // 2, "lo": n_node // 4, "hi": 4}


def span(sizes, order, phase):
    return math.prod(sizes[a] for a in order[phase + 1 :])


def parts_of(columns):
    return [(first, ORDER_B if i % 2 else ORDER_A) for i, first in enumerate(range(0, columns, LANES))]


def finish_kernel(n_node, n_rep, hot_base, g_ref, cold_ref, hot_ref, ids_ref, og, ocold, new_hot, *scratch):
    sizes = sizes_of(n_node, n_rep)
    parts = parts_of(g_ref.shape[2])
    send_sem, recv_sem = scratch[:2]
    buffers = scratch[2 : 2 + 8 * len(parts)]
    band, width = hot_ref.shape
    tidy = band % 8 == 0
    ohot, pieces = scratch[2 + 8 * len(parts) :] if tidy else (new_hot, None)
    node = lax.axis_index("node")
    rep = lax.axis_index("rep")
    nlo = sizes["lo"]
    mine = {"core": lax.rem(rep, 2), "x": lax.div(rep, 2), "lo": lax.rem(node, nlo), "hi": lax.div(node, nlo)}

    def peer(axis, k):
        spot = dict(mine)
        spot[axis] = lax.rem(mine[axis] + k, sizes[axis])
        return (spot["hi"] * nlo + spot["lo"], spot["x"] * 2 + spot["core"])

    greet([peer(axis, k) for axis in ORDER_A for k in range(1, sizes[axis])])

    everything = []

    def ship(src, dst, device):
        i = len(everything)
        copy = push(src, dst, send_sem.at[i], recv_sem.at[i], device)
        everything.append(copy)
        return copy

    def arrive(copies):
        for copy in copies:
            copy.wait_recv()

    def held(part, phase):
        first, order = parts[part]
        if phase == 0:
            return lambda i, n: g_ref.at[pl.ds(i, n), :, pl.ds(first, LANES)]
        acc = buffers[8 * part + 2 * (phase - 1) + 1]
        return lambda i, n: acc.at[pl.ds(i, n)]

    def scatter_start(part, phase):
        order = parts[part][1]
        axis = order[phase]
        size, n = sizes[axis], span(sizes, order, phase)
        view, recv = held(part, phase), buffers[8 * part + 2 * phase]
        return [
            ship(view(lax.rem(mine[axis] + k, size) * n, n), recv.at[k - 1], peer(axis, k)) for k in range(1, size)
        ]

    def scatter_end(part, phase, copies):
        order = parts[part][1]
        axis = order[phase]
        n = span(sizes, order, phase)
        recv, acc = buffers[8 * part + 2 * phase], buffers[8 * part + 2 * phase + 1]
        total = held(part, phase)(mine[axis] * n, n)[...]
        for k, copy in enumerate(copies):
            copy.wait_recv()
            total = total + recv[k]
        acc[...] = total

    def prefix(order, phase):
        return sum(mine[order[i]] * span(sizes, order, i) for i in range(phase + 1))

    def gather_start(part, phase):
        first, order = parts[part]
        axis = order[phase]
        where = og.at[pl.ds(prefix(order, phase), span(sizes, order, phase)), :, pl.ds(first, LANES)]
        return [ship(where, where, peer(axis, k)) for k in range(1, sizes[axis])]

    def hot_start(phase):
        axis = ORDER_HOT[phase]
        spot = [mine[a] if a in ORDER_HOT[: phase + 1] else slice(None) for a in ("hi", "lo", "x", "core")]
        where = ohot.at[tuple(spot)]
        return [ship(where, where, peer(axis, k)) for k in range(1, sizes[axis])]

    everyone = range(len(parts))
    flying = [scatter_start(part, 0) for part in everyone]
    ocold[mine["x"], mine["core"]] = cold_ref[...]
    ohot[mine["hi"], mine["lo"], mine["x"], mine["core"]] = hot_ref[...]
    cold_place = ocold.at[mine["x"], mine["core"]]
    hot_copies = hot_start(3)
    cold_copies = [ship(cold_place, cold_place, peer("x", k)) for k in range(1, sizes["x"])]

    for phase in range(4):
        for part in everyone:
            scatter_end(part, phase, flying[part])
            if phase < 3:
                flying[part] = scatter_start(part, phase + 1)
            else:
                first, order = parts[part]
                og[pl.ds(prefix(order, 3), 1), :, first : first + LANES] = buffers[8 * part + 7][...]
                flying[part] = gather_start(part, 3)
        arrive(hot_copies)
        hot_copies = hot_start(2 - phase) if phase < 3 else []
        if phase == 1:
            arrive(cold_copies)
            side = ocold.at[:, mine["core"]]
            cold_copies = [ship(side, side, peer("core", 1))]
    if tidy:
        hot_rows = new_hot.shape[0]
        rows = ohot[...].reshape(hot_rows, width)
        top = rows.astype(jnp.bfloat16)
        rest = rows - top.astype(jnp.float32)
        middle = rest.astype(jnp.bfloat16)
        pieces[:, :width] = top
        pieces[:, width : 2 * width] = middle
        pieces[:, 2 * width :] = (rest - middle.astype(jnp.float32)).astype(jnp.bfloat16)

    def permute_hot(part):
        step = new_hot.shape[0] // 4
        chosen = lax.broadcasted_iota(jnp.int32, (new_hot.shape[0], step), 0)
        chosen = chosen == ids_ref[:, part * step : (part + 1) * step] - hot_base
        got = lax.dot_general(
            jnp.where(chosen, 1.0, 0.0).astype(jnp.bfloat16),
            pieces[...],
            (((0,), (0,)), ((), ())),
            preferred_element_type=jnp.float32,
        )
        new_hot[part * step : (part + 1) * step] = got[:, :width] + got[:, width : 2 * width] + got[:, 2 * width :]

    for phase in (3, 2, 1, 0):
        for part in everyone:
            arrive(flying[part])
            flying[part] = gather_start(part, phase - 1) if phase else []
        if tidy:
            permute_hot(3 - phase)
    arrive(cold_copies)
    for copy in everything:
        copy.wait_send()


def finish(n_node, n_rep, hot_base, grads, cold, hot, ids):
    sizes = sizes_of(n_node, n_rep)
    f32 = jnp.float32
    n_dev, piece, columns = grads.shape
    parts = parts_of(columns)
    steps = sum(s - 1 for s in sizes.values())
    n_sems = 2 * steps * len(parts) + steps + sizes["x"] - 1 + 1
    scratch = [pltpu.SemaphoreType.DMA((n_sems,)), pltpu.SemaphoreType.DMA((n_sems,))]
    for first, order in parts:
        for phase in range(4):
            block = (span(sizes, order, phase), piece, LANES)
            scratch += [pltpu.VMEM((sizes[order[phase]] - 1, *block), f32), pltpu.VMEM(block, f32)]
    band, width = hot.shape
    hot_rows = ids.shape[1]
    blocks = (sizes["hi"], sizes["lo"], sizes["x"], 2, band, width)
    out_hot = jax.ShapeDtypeStruct(blocks, f32)
    if band % 8 == 0:
        out_hot = jax.ShapeDtypeStruct((hot_rows, width), f32)
        scratch += [pltpu.VMEM(blocks, f32), pltpu.VMEM((hot_rows, 3 * width), jnp.bfloat16)]
    return pl.pallas_call(
        functools.partial(finish_kernel, n_node, n_rep, hot_base),
        out_shape=(
            jax.ShapeDtypeStruct(grads.shape, f32),
            jax.ShapeDtypeStruct((sizes["x"], 2, *cold.shape), f32),
            out_hot,
        ),
        in_specs=[VMEM] * 4,
        out_specs=(VMEM,) * 3,
        scratch_shapes=scratch,
        compiler_params=pltpu.CompilerParams(
            collective_id=1, has_side_effects=True, vmem_limit_bytes=40 * 1024 * 1024
        ),
    )(grads, cold, hot, ids)


def on_device(
    memory,
    hot_memory,
    cot_cold,
    cot_hot,
    src_local,
    dst_ids,
    times,
    edge_feat,
    cold_list,
    cold_count,
    hot_ids,
    time_freq,
    time_phase,
    w_msg,
    b_msg,
    w_in,
    w_hid,
):
    f32, bf16 = jnp.float32, jnp.bfloat16
    n_node = lax.axis_size("node")
    n_rep = lax.axis_size("rep")
    n_dev = n_node * n_rep
    rows_dev, width = memory.shape
    hot_rows = hot_memory.shape[0]
    events = src_local.shape[0]
    msg_width = w_msg.shape[1]
    band = hot_rows // n_dev
    share = rows_dev // n_rep
    rep = lax.axis_index("rep")
    hot_base = n_node * rows_dev

    pick = (src_local[:, None] == jnp.arange(rows_dev, dtype=jnp.int32)[None, :]).astype(bf16)
    src_mem = jnp.dot(pick, memory.astype(bf16), preferred_element_type=f32).astype(bf16)
    enc = jnp.cos(times.astype(f32)[:, None] * time_freq[None, :] + time_phase[None, :]).astype(bf16)
    raw = jnp.concatenate([src_mem, edge_feat, enc], axis=1)
    messages = jax.nn.silu(jnp.dot(raw, w_msg, preferred_element_type=f32) + b_msg[None, :]).astype(bf16)

    ids_row = hot_ids.reshape(1, hot_rows)
    cold_total, cold_cnt, hot_sum, mem, cot = exchange(
        n_node,
        n_rep,
        messages,
        cold_list,
        cold_count.reshape(n_node, 1),
        dst_ids.reshape(1, events),
        ids_row,
        memory,
        cot_cold,
        hot_memory,
        cot_hot,
    )
    cold_number = lax.dynamic_index_in_dim(cold_cnt, rep, 0, keepdims=False)[0]
    total = jnp.concatenate([cold_total, hot_sum[:, :msg_width]], axis=0)
    count = jnp.concatenate([cold_number, hot_sum[:, msg_width]], axis=0)

    agg = (total / jnp.maximum(count, 1.0)[:, None]).astype(bf16)
    live = (count > 0)[:, None]
    gate_in = jnp.dot(agg, w_in, preferred_element_type=f32)
    mem_round = mem.astype(bf16)
    gate_hid = jnp.dot(mem_round, w_hid, preferred_element_type=f32)
    reset = jax.nn.sigmoid(gate_in[:, :width] + gate_hid[:, :width])
    update = jax.nn.sigmoid(gate_in[:, width : 2 * width] + gate_hid[:, width : 2 * width])
    hid_cand = gate_hid[:, 2 * width :]
    cand = jnp.tanh(gate_in[:, 2 * width :] + reset * hid_cand)
    fresh = jnp.where(live, (1.0 - update) * cand + update * mem, mem)
    cot = jnp.where(live, cot, 0.0)
    d_cand = cot * (1.0 - update) * (1.0 - cand * cand)
    d_upd = cot * (mem - cand) * update * (1.0 - update)
    d_reset = d_cand * hid_cand * reset * (1.0 - reset)
    d_input = jnp.concatenate([d_reset, d_upd, d_cand], axis=1) * GRAD_SCALE
    d_hidden = jnp.concatenate([d_reset, d_upd, d_cand * reset], axis=1) * GRAD_SCALE
    mem_wide = lax.optimization_barrier(mem_round).astype(f32)
    grad_a = jnp.dot(agg.astype(f32).T, d_input, precision=lax.Precision.HIGHEST)
    grad_b = jnp.dot(mem_wide.T, d_hidden, precision=lax.Precision.HIGHEST)
    grads = jnp.concatenate([grad_a, grad_b], axis=0)
    g_rows, g_cols = grads.shape
    grads, new_cold, new_hot = finish(
        n_node, n_rep, hot_base, grads.reshape(n_dev, g_rows // n_dev, g_cols), fresh[:share], fresh[share:], ids_row
    )
    grads = grads.reshape(g_rows, g_cols)
    agg_rows = w_in.shape[0]
    if band % 8:
        new_hot = jnp.take(new_hot.reshape(hot_rows, width), hot_ids - hot_base, axis=0)
    return (new_cold.reshape(rows_dev, width), new_hot, grads[:agg_rows], grads[agg_rows:])


def solution(mesh):
    both = P(("node", "rep"))
    in_specs = (
        P("node", None),
        P(),
        P("node", None),
        P(),
        both,
        both,
        both,
        P(("node", "rep"), None),
        P(("node", "rep"), None),
        both,
        P(),
        P(),
        P(),
        P(),
        P(),
        P(),
        P(),
    )
    out_specs = (P("node", None), P(), P(), P())
    return jax.shard_map(on_device, mesh=mesh, in_specs=in_specs, out_specs=out_specs, check_vma=False)
```

```python
import functools
import math

import jax
import jax.numpy as jnp
from jax import lax
from jax.experimental import pallas as pl
from jax.experimental.pallas import tpu as pltpu
from jax.sharding import PartitionSpec as P

GRAD_SCALE = 1.0 / 64.0
BANDS = 4
MESH = pl.DeviceIdType.MESH
VMEM = pl.BlockSpec(memory_space=pltpu.VMEM)


def greet(devices):
    barrier = pltpu.get_barrier_semaphore()
    for device in devices:
        pl.semaphore_signal(barrier, inc=1, device_id=device, device_id_type=MESH)
    pl.semaphore_wait(barrier, len(devices))


def push(src, dst, send_sem, recv_sem, device):
    copy = pltpu.make_async_remote_copy(
        src_ref=src, dst_ref=dst, send_sem=send_sem, recv_sem=recv_sem, device_id=device, device_id_type=MESH
    )
    copy.start()
    return copy


def exchange_kernel(
    n_node, n_rep,
    messages_ref, list_ref, number_ref, dst_ref, ids_ref, memory_any, cot_any, hot_memory_any, hot_cot_any,
    sum_out, cnt_out, hot_out, mem_out, cot_out,
    rows_ref, hot_ref, hot_state, own_sem,
    rows_recv, hot_recv, cnts, cnt_core, cnt_send, cnt_x,
    msg_s, msg_r, row_s, row_r, hot_s, hot_r, core_s, core_r, x_s, x_r, cc_s, cc_r, cx_s, cx_r,
    *chunked,
):
    nx = n_rep // 2
    n_dev = n_node * n_rep
    node = lax.axis_index("node")
    rep = lax.axis_index("rep")
    core = lax.rem(rep, 2)
    xi = lax.div(rep, 2)
    me = node * n_rep + rep
    cap = list_ref.shape[1]
    msg_width = messages_ref.shape[1]
    cuts = cuts_of(msg_width)
    msg_refs, recvs, sums, core_recv, x_send, x_recv = (
        chunked[i * len(cuts) : (i + 1) * len(cuts)] for i in range(6)
    )
    share = sum_out.shape[0]
    rows_dev = share * n_rep
    events = messages_ref.shape[0]
    hot_rows = ids_ref.shape[1]
    band = hot_rows // n_dev
    hot_base = n_node * rows_dev
    f32, bf16 = jnp.float32, jnp.bfloat16
    nlo = n_node // 4
    hi, lo = lax.div(node, nlo), lax.rem(node, nlo)
    steps = [(a, b) for a in (2, 1, 3, 0) for b in range(nlo) if a or b]

    def node_at(a, b):
        return lax.rem(hi + a, 4) * nlo + lax.rem(lo + b, nlo)

    first = pl.multiple_of(rep * share, share)
    own_copies = [
        pltpu.make_async_copy(src, dst, own_sem.at[i])
        for i, (src, dst) in enumerate(
            (
                (memory_any.at[pl.ds(first, share)], mem_out.at[pl.ds(0, share)]),
                (cot_any.at[pl.ds(first, share)], cot_out.at[pl.ds(0, share)]),
                (hot_memory_any, hot_state.at[0]),
                (hot_cot_any, hot_state.at[1]),
            )
        )
    ]
    for copy in own_copies:
        copy.start()

    def at_linear(k):
        other = lax.rem(me + k, n_dev)
        return (lax.div(other, n_rep), lax.rem(other, n_rep))

    other_core = (node, xi * 2 + 1 - core)

    def at_x(k):
        return (node, lax.rem(xi + k, nx) * 2 + core)

    greet(
        [(node_at(a, b), rep) for a, b in steps]
        + [other_core]
        + [at_x(k) for k in range(1, nx)]
        + [at_linear(j) for j in range(1, BANDS)]
        + [at_linear(n_dev - j) for j in range(1, BANDS)]
    )

    dst = dst_ref[...]
    local_row = lax.rem(dst, rows_dev)
    which = lax.broadcasted_iota(jnp.int32, (8, events), 0)
    high = lax.div(local_row, 32)
    digits = jnp.where(which == 0, high, jnp.where(which == 1, local_row - high * 32, 0))
    digits = digits.astype(f32).astype(bf16)
    slot = lax.broadcasted_iota(jnp.int32, (1, cap), 1)

    def build(other):
        listed = lax.broadcasted_iota(jnp.int32, (events, cap), 0) == list_ref[pl.ds(other, 1), :]
        listed = jnp.where(listed, 1.0, 0.0).astype(bf16)
        block = lax.dot_general(
            listed, messages_ref[...], (((0,), (0,)), ((), ())), preferred_element_type=f32
        ).astype(bf16)
        for ref, (begin, size) in zip(msg_refs, cuts):
            ref[other] = block[:, begin : begin + size]
        found = jnp.dot(digits, listed, preferred_element_type=f32)
        row = (found[0:1] * 32.0 + found[1:2]).astype(jnp.int32)
        mark = lax.broadcasted_iota(jnp.int32, (1, n_node), 1) == other
        number = jnp.sum(jnp.where(mark, number_ref[...], 0).astype(f32), axis=1, keepdims=True)
        row = jnp.where(slot.astype(f32) < number, row, -1)
        rows_ref[other, :, :cap] = jnp.broadcast_to(row, (8, cap))

    arrivals = {}
    for k, (a, b) in enumerate(steps):
        other = node_at(a, b)
        build(other)
        arrivals["row", k] = push(rows_ref.at[other], rows_recv.at[node], row_s.at[k], row_r.at[k], (other, rep))
        arrivals[0, k] = push(
            msg_refs[0].at[other], recvs[0].at[node], msg_s.at[0, k], msg_r.at[0, k], (other, rep)
        )
    for h in range(1, len(cuts)):
        for k, (a, b) in enumerate(steps):
            other = node_at(a, b)
            arrivals[h, k] = push(
                msg_refs[h].at[other], recvs[h].at[node], msg_s.at[h, k], msg_r.at[h, k], (other, rep)
            )
    sent = list(arrivals.values())

    place = dst - hot_base - me * band
    place = jnp.where(place < 0, place + hot_rows, place)
    place = jnp.where(dst >= hot_base, place, -1)
    match = jnp.where(lax.broadcasted_iota(jnp.int32, (BANDS * band, events), 0) == place, 1.0, 0.0)
    hot_part = jnp.dot(match.astype(bf16), messages_ref[...], preferred_element_type=f32)
    hot_number = jnp.sum(match, axis=1, keepdims=True)
    for j in range(BANDS):
        hot_ref[j, :, :msg_width] = hot_part[j * band : (j + 1) * band]
        hot_ref[j, :, msg_width:] = jnp.broadcast_to(hot_number[j * band : (j + 1) * band], (band, 128))
    hots = [
        push(hot_ref.at[j], hot_recv.at[j - 1], hot_s.at[j - 1], hot_r.at[j - 1], at_linear(j))
        for j in range(1, BANDS)
    ]
    sent += hots
    build(node)
    for copy in own_copies:
        copy.wait()
    own_rows = max(band, 8)
    own = lax.broadcasted_iota(jnp.int32, (own_rows, hot_rows), 0) + (hot_base + me * band) == ids_ref[...]
    own = jnp.where(own, 1.0, 0.0)
    for i, out in enumerate((mem_out, cot_out)):
        rows = jnp.dot(own, hot_state[i], precision=lax.Precision.HIGHEST, preferred_element_type=f32)
        out[share : share + band] = rows[:band]

    for ref in sums:
        ref[...] = jnp.zeros_like(ref)
    cnts[...] = jnp.zeros_like(cnts)
    ones = jnp.ones((8, cap), jnp.bfloat16)

    def add_block(h, rows, block):
        for s in range(n_rep):
            spot = lax.broadcasted_iota(jnp.int32, (share, cap), 0) + s * share
            equal = jnp.where(spot == rows, 1.0, 0.0).astype(jnp.bfloat16)
            sums[h][s // 2, s % 2] += jnp.dot(equal, block, preferred_element_type=jnp.float32)
            if h == 0:
                cnts[s] += lax.dot_general(
                    ones, equal, (((1,), (1,)), ((), ())), preferred_element_type=jnp.float32
                )

    crossing = [[] for _ in cuts]
    counts = []
    for h, (mine, got) in enumerate(zip(msg_refs, recvs)):
        add_block(h, rows_ref[node, 0:1, :cap], mine[node])
        for k, (a, b) in enumerate(steps):
            if h == 0:
                arrivals["row", k].wait_recv()
            arrivals[h, k].wait_recv()
            origin = node_at(4 - a, nlo - b)
            add_block(h, rows_recv[origin, 0:1, :cap], got[origin])
        halves = []
        for k in [*range(1, nx), 0]:
            p = lax.rem(xi + k, nx)
            copy = push(sums[h].at[p, 1 - core], core_recv[h].at[k], core_s.at[h, k], core_r.at[h, k], other_core)
            halves.append((k, p, copy))
        if h == 0:
            cnt_copy = push(cnts, cnt_core, cc_s, cc_r, other_core)
            sent.append(cnt_copy)
        for k, p, copy in halves:
            copy.wait_recv()
            sent.append(copy)
            if k:
                x_send[h][k - 1] = sums[h][p, core] + core_recv[h][k]
                crossing[h].append(
                    push(x_send[h].at[k - 1], x_recv[h].at[k - 1], x_s.at[h, k - 1], x_r.at[h, k - 1], at_x(k))
                )
        if h == 0:
            cnt_copy.wait_recv()
            cnt_send[...] = cnts[...] + cnt_core[...]
            counts = [
                push(cnt_send, cnt_x.at[k - 1], cx_s.at[k - 1], cx_r.at[k - 1], at_x(k)) for k in range(1, nx)
            ]
    for copy in hots:
        copy.wait_recv()
    hot_out[...] = hot_ref[0] + hot_recv[0] + hot_recv[1] + hot_recv[2]
    number = cnt_send[...]
    for k, copy in enumerate(counts):
        copy.wait_recv()
        number += cnt_x[k]
    cnt_out[...] = number
    for h, (begin, size) in enumerate(cuts):
        total = sums[h][xi, core] + core_recv[h][0]
        for k, copy in enumerate(crossing[h]):
            copy.wait_recv()
            total += x_recv[h][k]
        sum_out[:, begin : begin + size] = total
    for copy in [*sent, *sum(crossing, []), *counts]:
        copy.wait_send()


def cuts_of(width):
    return [(0, width // 2), (width // 2, width // 4), (3 * width // 4, width // 4)]


def exchange(n_node, n_rep, messages, lists, numbers, dst, ids, memory, cot, hot_memory, hot_cot):
    nx = n_rep // 2
    cap = lists.shape[1]
    msg_width = messages.shape[1]
    cuts = cuts_of(msg_width)
    rows_dev, width = memory.shape
    hot_rows = hot_memory.shape[0]
    band = hot_rows // (n_node * n_rep)
    hot_width = msg_width + 128
    share = rows_dev // n_rep
    dma = pltpu.SemaphoreType.DMA
    f32 = jnp.float32

    def chunked(*shape, dtype=jnp.float32):
        return [pltpu.VMEM((*shape, size), dtype) for _, size in cuts]

    row_block = pltpu.VMEM((n_node, 8, 128), jnp.int32)
    return pl.pallas_call(
        functools.partial(exchange_kernel, n_node, n_rep),
        out_shape=(
            jax.ShapeDtypeStruct((share, msg_width), f32),
            jax.ShapeDtypeStruct((n_rep, 8, share), f32),
            jax.ShapeDtypeStruct((band, hot_width), f32),
            jax.ShapeDtypeStruct((share + band, width), f32),
            jax.ShapeDtypeStruct((share + band, width), f32),
        ),
        in_specs=[VMEM] * 5 + [pl.BlockSpec(memory_space=pl.ANY)] * 4,
        out_specs=(VMEM,) * 5,
        scratch_shapes=[
            row_block,
            pltpu.VMEM((BANDS, band, hot_width), f32),
            pltpu.VMEM((2, hot_rows, width), f32),
            dma((4,)),
            row_block,
            pltpu.VMEM((BANDS - 1, band, hot_width), f32),
            pltpu.VMEM((n_rep, 8, share), f32),
            pltpu.VMEM((n_rep, 8, share), f32),
            pltpu.VMEM((n_rep, 8, share), f32),
            pltpu.VMEM((nx - 1, n_rep, 8, share), f32),
            dma((len(cuts), n_node)), dma((len(cuts), n_node)), dma((n_node,)), dma((n_node,)),
            dma((BANDS - 1,)), dma((BANDS - 1,)),
            dma((len(cuts), nx)), dma((len(cuts), nx)),
            dma((len(cuts), nx - 1)), dma((len(cuts), nx - 1)),
            dma, dma,
            dma((nx - 1,)), dma((nx - 1,)),
            *chunked(n_node, cap, dtype=messages.dtype),
            *chunked(n_node, cap, dtype=messages.dtype),
            *chunked(nx, 2, share),
            *chunked(nx, share),
            *chunked(nx - 1, share),
            *chunked(nx - 1, share),
        ],
        compiler_params=pltpu.CompilerParams(
            collective_id=0, has_side_effects=True, vmem_limit_bytes=40 * 1024 * 1024
        ),
    )(messages, lists, numbers, dst, ids, memory, cot, hot_memory, hot_cot)


ORDER_A = ("core", "x", "lo", "hi")
ORDER_B = ("core", "lo", "x", "hi")
ORDER_HOT = ("core", "lo", "hi", "x")
LANES = 128


def sizes_of(n_node, n_rep):
    return {"core": 2, "x": n_rep // 2, "lo": n_node // 4, "hi": 4}


def span(sizes, order, phase):
    return math.prod(sizes[a] for a in order[phase + 1 :])


def parts_of(columns):
    return [(first, ORDER_B if i % 2 else ORDER_A) for i, first in enumerate(range(0, columns, LANES))]


def finish_kernel(n_node, n_rep, hot_base, g_ref, cold_ref, hot_ref, ids_ref, og, ocold, new_hot, *scratch):
    sizes = sizes_of(n_node, n_rep)
    parts = parts_of(g_ref.shape[2])
    send_sem, recv_sem = scratch[:2]
    buffers = scratch[2 : 2 + 8 * len(parts)]
    band, width = hot_ref.shape
    tidy = band % 8 == 0
    ohot, pieces = scratch[2 + 8 * len(parts) :] if tidy else (new_hot, None)
    node = lax.axis_index("node")
    rep = lax.axis_index("rep")
    nlo = sizes["lo"]
    mine = {"core": lax.rem(rep, 2), "x": lax.div(rep, 2), "lo": lax.rem(node, nlo), "hi": lax.div(node, nlo)}

    def peer(axis, k):
        spot = dict(mine)
        spot[axis] = lax.rem(mine[axis] + k, sizes[axis])
        return (spot["hi"] * nlo + spot["lo"], spot["x"] * 2 + spot["core"])

    greet([peer(axis, k) for axis in ORDER_A for k in range(1, sizes[axis])])

    everything = []

    def ship(src, dst, device):
        i = len(everything)
        copy = push(src, dst, send_sem.at[i], recv_sem.at[i], device)
        everything.append(copy)
        return copy

    def arrive(copies):
        for copy in copies:
            copy.wait_recv()

    def held(part, phase):
        first, order = parts[part]
        if phase == 0:
            return lambda i, n: g_ref.at[pl.ds(i, n), :, pl.ds(first, LANES)]
        acc = buffers[8 * part + 2 * (phase - 1) + 1]
        return lambda i, n: acc.at[pl.ds(i, n)]

    def scatter_start(part, phase):
        order = parts[part][1]
        axis = order[phase]
        size, n = sizes[axis], span(sizes, order, phase)
        view, recv = held(part, phase), buffers[8 * part + 2 * phase]
        return [
            ship(view(lax.rem(mine[axis] + k, size) * n, n), recv.at[k - 1], peer(axis, k)) for k in range(1, size)
        ]

    def scatter_end(part, phase, copies):
        order = parts[part][1]
        axis = order[phase]
        n = span(sizes, order, phase)
        recv, acc = buffers[8 * part + 2 * phase], buffers[8 * part + 2 * phase + 1]
        total = held(part, phase)(mine[axis] * n, n)[...]
        for k, copy in enumerate(copies):
            copy.wait_recv()
            total = total + recv[k]
        acc[...] = total

    def prefix(order, phase):
        return sum(mine[order[i]] * span(sizes, order, i) for i in range(phase + 1))

    def gather_start(part, phase):
        first, order = parts[part]
        axis = order[phase]
        where = og.at[pl.ds(prefix(order, phase), span(sizes, order, phase)), :, pl.ds(first, LANES)]
        return [ship(where, where, peer(axis, k)) for k in range(1, sizes[axis])]

    def hot_start(phase):
        axis = ORDER_HOT[phase]
        spot = [mine[a] if a in ORDER_HOT[: phase + 1] else slice(None) for a in ("hi", "lo", "x", "core")]
        where = ohot.at[tuple(spot)]
        return [ship(where, where, peer(axis, k)) for k in range(1, sizes[axis])]

    everyone = range(len(parts))
    flying = [scatter_start(part, 0) for part in everyone]
    ocold[mine["x"], mine["core"]] = cold_ref[...]
    ohot[mine["hi"], mine["lo"], mine["x"], mine["core"]] = hot_ref[...]
    cold_place = ocold.at[mine["x"], mine["core"]]
    hot_copies = hot_start(3)
    cold_copies = [ship(cold_place, cold_place, peer("x", k)) for k in range(1, sizes["x"])]

    for phase in range(4):
        for part in everyone:
            scatter_end(part, phase, flying[part])
            if phase < 3:
                flying[part] = scatter_start(part, phase + 1)
            else:
                first, order = parts[part]
                og[pl.ds(prefix(order, 3), 1), :, first : first + LANES] = buffers[8 * part + 7][...]
                flying[part] = gather_start(part, 3)
        arrive(hot_copies)
        hot_copies = hot_start(2 - phase) if phase < 3 else []
        if phase == 1:
            arrive(cold_copies)
            side = ocold.at[:, mine["core"]]
            cold_copies = [ship(side, side, peer("core", 1))]
    if tidy:
        hot_rows = new_hot.shape[0]
        rows = ohot[...].reshape(hot_rows, width)
        top = rows.astype(jnp.bfloat16)
        rest = rows - top.astype(jnp.float32)
        middle = rest.astype(jnp.bfloat16)
        pieces[:, :width] = top
        pieces[:, width : 2 * width] = middle
        pieces[:, 2 * width :] = (rest - middle.astype(jnp.float32)).astype(jnp.bfloat16)

    def permute_hot(part):
        step = new_hot.shape[0] // 4
        chosen = lax.broadcasted_iota(jnp.int32, (new_hot.shape[0], step), 0)
        chosen = chosen == ids_ref[:, part * step : (part + 1) * step] - hot_base
        got = lax.dot_general(
            jnp.where(chosen, 1.0, 0.0).astype(jnp.bfloat16),
            pieces[...],
            (((0,), (0,)), ((), ())),
            preferred_element_type=jnp.float32,
        )
        new_hot[part * step : (part + 1) * step] = got[:, :width] + got[:, width : 2 * width] + got[:, 2 * width :]

    for phase in (3, 2, 1, 0):
        for part in everyone:
            arrive(flying[part])
            flying[part] = gather_start(part, phase - 1) if phase else []
        if tidy:
            permute_hot(3 - phase)
    arrive(cold_copies)
    for copy in everything:
        copy.wait_send()


def finish(n_node, n_rep, hot_base, grads, cold, hot, ids):
    sizes = sizes_of(n_node, n_rep)
    f32 = jnp.float32
    n_dev, piece, columns = grads.shape
    parts = parts_of(columns)
    steps = sum(s - 1 for s in sizes.values())
    n_sems = 2 * steps * len(parts) + steps + sizes["x"] - 1 + 1
    scratch = [pltpu.SemaphoreType.DMA((n_sems,)), pltpu.SemaphoreType.DMA((n_sems,))]
    for first, order in parts:
        for phase in range(4):
            block = (span(sizes, order, phase), piece, LANES)
            scratch += [pltpu.VMEM((sizes[order[phase]] - 1, *block), f32), pltpu.VMEM(block, f32)]
    band, width = hot.shape
    hot_rows = ids.shape[1]
    blocks = (sizes["hi"], sizes["lo"], sizes["x"], 2, band, width)
    out_hot = jax.ShapeDtypeStruct(blocks, f32)
    if band % 8 == 0:
        out_hot = jax.ShapeDtypeStruct((hot_rows, width), f32)
        scratch += [pltpu.VMEM(blocks, f32), pltpu.VMEM((hot_rows, 3 * width), jnp.bfloat16)]
    return pl.pallas_call(
        functools.partial(finish_kernel, n_node, n_rep, hot_base),
        out_shape=(
            jax.ShapeDtypeStruct(grads.shape, f32),
            jax.ShapeDtypeStruct((sizes["x"], 2, *cold.shape), f32),
            out_hot,
        ),
        in_specs=[VMEM] * 4,
        out_specs=(VMEM,) * 3,
        scratch_shapes=scratch,
        compiler_params=pltpu.CompilerParams(
            collective_id=1, has_side_effects=True, vmem_limit_bytes=40 * 1024 * 1024
        ),
    )(grads, cold, hot, ids)


def on_device(
    memory,
    hot_memory,
    cot_cold,
    cot_hot,
    src_local,
    dst_ids,
    times,
    edge_feat,
    cold_list,
    cold_count,
    hot_ids,
    time_freq,
    time_phase,
    w_msg,
    b_msg,
    w_in,
    w_hid,
):
    f32, bf16 = jnp.float32, jnp.bfloat16
    n_node = lax.axis_size("node")
    n_rep = lax.axis_size("rep")
    n_dev = n_node * n_rep
    rows_dev, width = memory.shape
    hot_rows = hot_memory.shape[0]
    events = src_local.shape[0]
    msg_width = w_msg.shape[1]
    band = hot_rows // n_dev
    share = rows_dev // n_rep
    rep = lax.axis_index("rep")
    hot_base = n_node * rows_dev

    pick = (src_local[:, None] == jnp.arange(rows_dev, dtype=jnp.int32)[None, :]).astype(bf16)
    src_mem = jnp.dot(pick, memory.astype(bf16), preferred_element_type=f32).astype(bf16)
    enc = jnp.cos(times.astype(f32)[:, None] * time_freq[None, :] + time_phase[None, :]).astype(bf16)
    raw = jnp.concatenate([src_mem, edge_feat, enc], axis=1)
    messages = jax.nn.silu(jnp.dot(raw, w_msg, preferred_element_type=f32) + b_msg[None, :]).astype(bf16)

    ids_row = hot_ids.reshape(1, hot_rows)
    cold_total, cold_cnt, hot_sum, mem, cot = exchange(
        n_node,
        n_rep,
        messages,
        cold_list,
        cold_count.reshape(1, n_node),
        dst_ids.reshape(1, events),
        ids_row,
        memory,
        cot_cold,
        hot_memory,
        cot_hot,
    )
    cold_number = lax.dynamic_index_in_dim(cold_cnt, rep, 0, keepdims=False)[0]
    total = jnp.concatenate([cold_total, hot_sum[:, :msg_width]], axis=0)
    count = jnp.concatenate([cold_number, hot_sum[:, msg_width]], axis=0)

    agg = (total / jnp.maximum(count, 1.0)[:, None]).astype(bf16)
    live = (count > 0)[:, None]
    gate_in = jnp.dot(agg, w_in, preferred_element_type=f32)
    mem_round = mem.astype(bf16)
    gate_hid = jnp.dot(mem_round, w_hid, preferred_element_type=f32)
    reset = jax.nn.sigmoid(gate_in[:, :width] + gate_hid[:, :width])
    update = jax.nn.sigmoid(gate_in[:, width : 2 * width] + gate_hid[:, width : 2 * width])
    hid_cand = gate_hid[:, 2 * width :]
    cand = jnp.tanh(gate_in[:, 2 * width :] + reset * hid_cand)
    fresh = jnp.where(live, (1.0 - update) * cand + update * mem, mem)
    cot = jnp.where(live, cot, 0.0)
    d_cand = cot * (1.0 - update) * (1.0 - cand * cand)
    d_upd = cot * (mem - cand) * update * (1.0 - update)
    d_reset = d_cand * hid_cand * reset * (1.0 - reset)
    d_input = jnp.concatenate([d_reset, d_upd, d_cand], axis=1) * GRAD_SCALE
    d_hidden = jnp.concatenate([d_reset, d_upd, d_cand * reset], axis=1) * GRAD_SCALE
    mem_wide = lax.optimization_barrier(mem_round).astype(f32)
    grad_a = jnp.dot(agg.astype(f32).T, d_input, precision=lax.Precision.HIGHEST)
    grad_b = jnp.dot(mem_wide.T, d_hidden, precision=lax.Precision.HIGHEST)
    grads = jnp.concatenate([grad_a, grad_b], axis=0)
    g_rows, g_cols = grads.shape
    grads, new_cold, new_hot = finish(
        n_node, n_rep, hot_base, grads.reshape(n_dev, g_rows // n_dev, g_cols), fresh[:share], fresh[share:], ids_row
    )
    grads = grads.reshape(g_rows, g_cols)
    agg_rows = w_in.shape[0]
    if band % 8:
        new_hot = jnp.take(new_hot.reshape(hot_rows, width), hot_ids - hot_base, axis=0)
    return (new_cold.reshape(rows_dev, width), new_hot, grads[:agg_rows], grads[agg_rows:])


def solution(mesh):
    both = P(("node", "rep"))
    in_specs = (
        P("node", None),
        P(),
        P("node", None),
        P(),
        both,
        both,
        both,
        P(("node", "rep"), None),
        P(("node", "rep"), None),
        both,
        P(),
        P(),
        P(),
        P(),
        P(),
        P(),
        P(),
    )
    out_specs = (P("node", None), P(), P(), P())
    return jax.shard_map(on_device, mesh=mesh, in_specs=in_specs, out_specs=out_specs, check_vma=False)
```
